32 devices in a mesh: dp: 8 (over z, x), tensor: 4 (over y, core).
Axes of the slice: x: 2, y: 2, z: 4, core: 2. Of those that a mesh axis runs over, the one named last changes fastest.
Arguments:
- layer_input: bfloat16 [32768, 512], P(('dp', 'tensor')), may hold values from -6 to 6
- lengths: int32 [8, 32, 2], P('dp'), may hold values from 0 to 126, as said below
- ln1_gain: float32 [512], replicated, may hold values from 0.5 to 1.5
- ln1_bias: float32 [512], replicated, may hold values from -3 to 3
- w_query: bfloat16 [512, 512], P(None, 'tensor'), may hold values from -0.25 to 0.25
- b_query: bfloat16 [512], P('tensor'), may hold values from -3 to 3
- w_key: bfloat16 [512, 512], P(None, 'tensor'), may hold values from -0.25 to 0.25
- w_value: bfloat16 [512, 512], P(None, 'tensor'), may hold values from -0.25 to 0.25
- b_value: bfloat16 [512], P('tensor'), may hold values from -3 to 3
- w_out: bfloat16 [512, 512], P('tensor'), may hold values from -0.75 to 0.75
- b_out: bfloat16 [512], replicated, may hold values from -3 to 3
- ln2_gain: float32 [512], replicated, may hold values from 0.5 to 1.5
- ln2_bias: float32 [512], replicated, may hold values from -3 to 3
- w_up: bfloat16 [512, 2048], P(None, 'tensor'), may hold values from -0.25 to 0.25
- b_up: bfloat16 [2048], P('tensor'), may hold values from -3 to 3
- w_down: bfloat16 [2048, 512], P('tensor'), may hold values from -0.125 to 0.125
- b_down: bfloat16 [512], replicated, may hold values from -3 to 3
- cotangent: bfloat16 [32768, 512], P(('dp', 'tensor')), may hold values from -6 to 6
Outputs:
- block_output: bfloat16 [32768, 512], P(('dp', 'tensor'))
- input_grad: bfloat16 [32768, 512], P(('dp', 'tensor'))
- grad_ln1_gain: float32 [512], replicated
- grad_ln1_bias: float32 [512], replicated
- grad_w_query: float32 [512, 512], P(None, 'tensor')
- grad_b_query: float32 [512], P('tensor')
- grad_w_key: float32 [512, 512], P(None, 'tensor')
- grad_w_value: float32 [512, 512], P(None, 'tensor')
- grad_b_value: float32 [512], P('tensor')
- grad_w_out: float32 [512, 512], P('tensor')
- grad_b_out: float32 [512], replicated
- grad_ln2_gain: float32 [512], replicated
- grad_ln2_bias: float32 [512], replicated
- grad_w_up: float32 [512, 2048], P(None, 'tensor')
- grad_b_up: float32 [2048], P('tensor')
- grad_w_down: float32 [2048, 512], P('tensor')
- grad_b_down: float32 [512], replicated
The draws below stay inside these ranges and needn't reach their ends.
Inputs may be any that keep to these rules, and one draw needn't show every extreme that they name: `lengths`: in each group the occupied slots come first, between 28 and 31 of them; the other slots hold 0 in both entries. In a group of 126-token sequences each occupied slot holds (126, 0); in a group of 48-token sequences each occupied slot holds (48, 48). Some group holds 126-token sequences and some other group 48-token ones.
All inputs are finite; a program needn't handle non-finite values.
Results may differ from the reference program's by a relative error of at most 0.018.
Values may be sent and summed in bfloat16 or wider, within the bound.
No kernel may reach another device: no remote copies, remote signals or barrier semaphores. Data moves between devices by JAX's collectives and lax.ppermute only.
A program may use at most 128 MiB of HBM per device.

```python
import math
import jax
import jax.numpy as jnp
from jax import lax

D = 512
HEADS = 8
HD = 64
FF = 2048
SLOTS = 32
SLOT = 128
SHORT = 48
LONG = 126
FRAME = 6
GROUPS = 8
TOKENS = 32768


def draw_lengths(key, part):
    key = jax.random.fold_in(key, 7)
    kind_key, count_key, order_key = jax.random.split(key, 3)
    seq_kinds = jax.random.randint(kind_key, (GROUPS,), 0, 2)
    group_order = jax.random.permutation(order_key, GROUPS)
    seq_kinds = jnp.where(group_order == 0, 1, jnp.where(group_order == 1, 0, seq_kinds))
    counts = jax.random.randint(count_key, (GROUPS,), SLOTS * 7 // 8, SLOTS)
    first_len = jnp.where(seq_kinds == 1, LONG, SHORT)
    second_len = jnp.where(seq_kinds == 1, 0, SHORT)
    places = jnp.arange(SLOTS)
    used = places[None, :] < counts[:, None]
    first = jnp.where(used, first_len[:, None], 0)
    second = jnp.where(used, second_len[:, None], 0)
    return jnp.stack([first, second], -1).astype(jnp.int32)


def level_of(own_key, extent, shards, smallest, top_value):
    level, own = 1.0, jax.random.fold_in(own_key, 6)
    for dim, parts in shards:
        steps = jnp.exp(jax.random.uniform(jax.random.fold_in(own, dim), (parts,), jnp.float32, smallest / len(shards), top_value / len(shards)))
        level = level * jnp.repeat(steps, extent[dim] // parts).reshape([-1 if axis == dim else 1 for axis in range(len(extent))])
    return level


def gaussian(key, extent, scale, most, pieces=(), held_as=jnp.bfloat16):
    result = jax.random.normal(key, extent, jnp.float32) * scale
    if len(pieces) > 0:
        result = level_of(key, extent, pieces, -0.22, 0.18) * result
    return jnp.clip(result, min=-most, max=most).astype(held_as)


def setup_inputs(seed: int = 0) -> dict:
    streams_of = jax.random.split(jax.random.key(seed), 19)
    return {
        "layer_input": gaussian(streams_of[0], (TOKENS, D), 1.0, 6.0, ((0, 32),)),
        "lengths": draw_lengths(jax.random.fold_in(streams_of[18], 71), 0),
        "ln1_gain": jnp.clip(1.0 + 0.1 * jax.random.normal(streams_of[2], (D,), jnp.float32), 0.5, 1.5),
        "ln1_bias": gaussian(streams_of[3], (D,), 0.5, 3.0, (), jnp.float32),
        "w_query": gaussian(streams_of[4], (D, HEADS * HD), D ** -0.5, 0.25, ((1, 4),)),
        "b_query": gaussian(streams_of[5], (HEADS * HD,), 0.5, 3.0, ((0, 4),)),
        "w_key": gaussian(streams_of[6], (D, HEADS * HD), D ** -0.5, 0.25, ((1, 4),)),
        "w_value": gaussian(streams_of[7], (D, HEADS * HD), D ** -0.5, 0.25, ((1, 4),)),
        "b_value": gaussian(streams_of[8], (HEADS * HD,), 0.5, 3.0, ((0, 4),)),
        "w_out": gaussian(streams_of[9], (HEADS * HD, D), (D // 8) ** -0.5, 0.75, ((0, 4),)),
        "b_out": gaussian(streams_of[10], (D,), 0.5, 3.0),
        "ln2_gain": jnp.clip(1.0 + 0.1 * jax.random.normal(streams_of[11], (D,), jnp.float32), 0.5, 1.5),
        "ln2_bias": gaussian(streams_of[12], (D,), 0.5, 3.0, (), jnp.float32),
        "w_up": gaussian(streams_of[13], (D, FF), D ** -0.5, 0.25, ((1, 4),)),
        "b_up": gaussian(streams_of[14], (FF,), 0.5, 3.0, ((0, 4),)),
        "w_down": gaussian(streams_of[15], (FF, D), FF ** -0.5, 0.125, ((0, 4),)),
        "b_down": gaussian(streams_of[16], (D,), 0.5, 3.0),
        "cotangent": gaussian(streams_of[17], (TOKENS, D), 1.0, 6.0, ((0, 32),)),
    }


norm_eps = 1e-05
highest = lax.Precision.HIGHEST

@jax.custom_vjp
def low(v):
    return lax.optimization_barrier(v.astype(jnp.bfloat16)).astype(jnp.float32)

@jax.custom_vjp
def low_back(v):
    return v

def low_keep(v):
    return (low(v), None)

def low_pass(kept, grad):
    return (grad,)

def back_keep(v):
    return (v, None)

def back_low(kept, grad):
    return (low(grad),)
low.defvjp(low_keep, low_pass)
low_back.defvjp(back_keep, back_low)

def layer_norm(values, gain, bias):
    row_mean = lax.optimization_barrier(jnp.mean(values, -1, keepdims=True))
    centred = values - row_mean
    variance = lax.optimization_barrier(jnp.mean(centred * centred, -1, keepdims=True))
    return centred * lax.rsqrt(variance + norm_eps) * gain + bias

def matmul(left, right):
    return jnp.dot(left, right, precision=highest)

def slot_masks(slot_lengths):
    places = jnp.arange(SLOT, dtype=jnp.int32)
    half_slot = SLOT // 2
    first_len = slot_lengths[:, 0:1]
    second_len = slot_lengths[:, 1:2]
    in_second = (second_len > 0) & (places[None, :] >= half_slot)
    local_pos = places[None, :] - jnp.where(in_second, half_slot, 0).astype(jnp.int32)
    is_valid = jnp.where(in_second, local_pos < second_len, places[None, :] < first_len)
    frames = local_pos // FRAME
    causal = frames[:, None, :] <= frames[:, :, None]
    same_seq = in_second[:, :, None] == in_second[:, None, :]
    allowed = is_valid[:, None, :] & is_valid[:, :, None] & causal & same_seq
    return (allowed[:, None], is_valid[:, None, :, None])

def attend_block(inputs):
    queries, key_rows, values, slot_lengths = inputs
    scores = low_back(jnp.einsum('bqhd,bkhd->bhqk', queries, key_rows, precision=highest) * HD ** (-0.5))
    allowed, valid_query = slot_masks(slot_lengths)
    row_top = lax.optimization_barrier(jnp.max(jnp.where(allowed, scores, -1e+30), -1, keepdims=True))
    row_top = jnp.where(valid_query, row_top, 0.0)
    expo_terms = jnp.where(allowed, jnp.exp(scores - row_top), 0.0)
    denom_sum = lax.optimization_barrier(jnp.sum(expo_terms, -1, keepdims=True)) + jnp.where(valid_query, 0.0, 1.0)
    softmax_w = low(expo_terms / denom_sum)
    return jnp.einsum('bhqk,bkhd->bqhd', softmax_w, values, precision=highest)

def layer(param_set, row_block, slot_lengths):
    ln1_gain, ln1_bias, w_query, b_query, w_key, w_value, b_value, w_out, b_out, ln2_gain, ln2_bias, w_up, b_up, w_down, b_down = param_set
    slot_count = slot_lengths.shape[0]
    per_block = math.gcd(slot_count, 4)
    block_shape = (slot_count // per_block, per_block, SLOT, HEADS, HD)
    normed_one = low(layer_norm(row_block, ln1_gain, ln1_bias))
    queries = low(low_back(matmul(normed_one, w_query) + b_query))
    key_rows = low(low_back(matmul(normed_one, w_key)))
    values = low(low_back(matmul(normed_one, w_value) + b_value))
    attended = lax.map(jax.checkpoint(attend_block), (queries.reshape(block_shape), key_rows.reshape(block_shape), values.reshape(block_shape), slot_lengths.reshape(slot_count // per_block, per_block, 2)))
    attended = low(low_back(attended.reshape(row_block.shape[0], HEADS * HD)))
    hidden_in = row_block + low_back(matmul(attended, w_out) + b_out)
    normed_two = low(layer_norm(hidden_in, ln2_gain, ln2_bias))
    up_rows = low_back(matmul(normed_two, w_up) + b_up)
    activated = low(jax.nn.gelu(up_rows, approximate=False))
    return hidden_in + low_back(matmul(activated, w_down) + b_down)

def reference(layer_input, lengths, ln1_gain, ln1_bias, w_query, b_query, w_key, w_value, b_value, w_out, b_out, ln2_gain, ln2_bias, w_up, b_up, w_down, b_down, cotangent):
    param_set = tuple((member.astype(jnp.float32) for member in (ln1_gain, ln1_bias, w_query, b_query, w_key, w_value, b_value, w_out, b_out, ln2_gain, ln2_bias, w_up, b_up, w_down, b_down)))
    group_count = lengths.shape[0]
    group_rows = lengths.shape[1] * SLOT
    inputs_grouped = layer_input.astype(jnp.float32).reshape(group_count, group_rows, D)
    cot_grouped = cotangent.astype(jnp.float32).reshape(group_count, group_rows, D)

    def one_group(running_sum, packed):
        row_block, slot_lengths, grad_out = packed
        outputs, pullback = jax.vjp(lambda params_in, rows_in: layer(params_in, rows_in, slot_lengths), param_set, row_block)
        grad_params, grad_rows = pullback(grad_out)
        running_sum = jax.tree.map(lambda running, addend: running + addend, running_sum, grad_params)
        return (running_sum, (outputs.astype(jnp.bfloat16), grad_rows.astype(jnp.bfloat16)))
    grad_zero = jax.tree.map(jnp.zeros_like, param_set)
    grad_sums, (outputs, grad_rows) = lax.scan(one_group, grad_zero, (inputs_grouped, lengths, cot_grouped))
    return (outputs.reshape(-1, D), grad_rows.reshape(-1, D), grad_sums[0], grad_sums[1], grad_sums[2], grad_sums[3], grad_sums[4], grad_sums[5], grad_sums[6], grad_sums[7], grad_sums[8], grad_sums[9], grad_sums[10], grad_sums[11], grad_sums[12], grad_sums[13], grad_sums[14])
```

```python
import functools

import jax
import jax.numpy as jnp
from jax import lax
from jax.experimental import pallas as pl
from jax.experimental.pallas import tpu as pltpu
from jax.sharding import PartitionSpec as P

BF, F32 = jnp.bfloat16, jnp.float32
D = 512
HD = 64
SLOT = 128
BR = 256
BIAS = 16
EPS = 1e-5
SLOT_UNROLL = 2
SMEM = functools.partial(pl.BlockSpec, memory_space=pltpu.SMEM)
VMEM = functools.partial(pl.BlockSpec, memory_space=pltpu.VMEM)


def dot(a, b):
    return lax.dot_general(a, b, (((1,), (0,)), ((), ())), preferred_element_type=F32)


def dot_nt(a, b):
    return lax.dot_general(a, b, (((1,), (1,)), ((), ())), preferred_element_type=F32)


def params(mib, **kw):
    return pltpu.CompilerParams(vmem_limit_bytes=mib << 20, **kw)


def cost(flops, nbytes, trans=0):
    return pl.CostEstimate(flops=int(flops), bytes_accessed=int(nbytes), transcendentals=int(trans))


def sds(shape, dtype=BF):
    return jax.ShapeDtypeStruct(shape, dtype)


def whole(shape):
    return pl.BlockSpec(shape, lambda *i: (0,) * len(shape))


def normalise(v):
    mean = jnp.mean(v, -1, keepdims=True)
    centred = v - mean
    rstd = lax.rsqrt(jnp.mean(centred * centred, -1, keepdims=True) + EPS)
    return centred * rstd, rstd


def head_stack(v):
    first = lax.broadcasted_iota(jnp.int32, v.shape, 1) < HD
    zero = jnp.zeros_like(v)
    return jnp.concatenate([jnp.where(first, v, zero), jnp.where(first, zero, v)], 0)


def untranspose(v):
    return jnp.concatenate([v[:, :SLOT].T, v[:, SLOT:].T], 1)


def slot_bias(len1, len2):
    def places(shape, dim):
        p = lax.broadcasted_iota(jnp.int32, shape, dim) & (SLOT - 1)
        second = (p >= SLOT // 2) & (len2 > 0)
        local = jnp.where(second, p - SLOT // 2, p)
        valid = local < jnp.where(second, len2, len1)
        base = jnp.where(second, 1000, 0)
        return valid, base, base + ((local * 43) >> 8)

    valid_k, _, frame_k = places((SLOT, 1), 0)
    valid_q, base_q, frame_q = places((1, 2 * SLOT), 1)
    frame_k = jnp.where(valid_k, frame_k, 1 << 20)
    frame_q = jnp.where(valid_q, frame_q, -1)
    allowed = (frame_k <= frame_q) & (frame_k >= base_q)
    return jnp.where(allowed, 0.0, -1e30).astype(F32)


def pack_kernel(wq, wk, wv, wo, bq, bv, bup, out):
    for i, ref in enumerate((wq, wk, wv)):
        out[0:D, i * 128 : (i + 1) * 128] = ref[...]
    for b in range(4):
        out[b * 128 : (b + 1) * 128, 384:512] = wo[:, b * 128 : (b + 1) * 128]
    zero = jnp.zeros((1, 128), F32)
    first = jnp.concatenate([bq[...].astype(F32), zero, bv[...].astype(F32), zero], 1)
    row = lax.broadcasted_iota(jnp.int32, (BIAS, D), 0)
    block = jnp.where(row == 0, first, jnp.where(row == 1, bup[...].astype(F32), 0.0))
    out[D : D + BIAS, :] = block.astype(BF)


def prep_kernel(x, gain, bias, bout, cot, n1_o, n1t_o, cott_o, base_o):
    def tile(m, _):
        here = pl.ds(pl.multiple_of(m * BR, BR), BR)
        xf = x[here, :].astype(F32)
        xhat, _ = normalise(xf)
        n1 = (xhat * gain[...] + bias[...]).astype(BF)
        n1_o[here, :] = n1
        n1t_o[:, here] = n1.T
        cott_o[:, here] = cot[here, :].T
        base_o[here, :] = xf + bout[...].astype(F32)
        return 0

    lax.fori_loop(0, x.shape[0] // BR, tile, 0)


def attn_fwd_kernel(last, *refs):
    if last:
        (scal, lens, n1, base, wa, wb, gain, bias, q_o, k_o, v_o, att_o, pt_o, hid_o, n2_o, n2t_o) = refs
    else:
        (scal, lens, n1, base, wa, wb, q_o, k_o, v_o, att_o, pt_o, hid_o) = refs
    slots = n1.shape[0] // SLOT

    for c, w in enumerate((wa, wb)):
        brow = w[D : D + BIAS, :].astype(F32)[0:1]
        cols = slice(c * 128, (c + 1) * 128)
        qkv = dot(n1[...], w[0:D, 0:384])
        q_o[:, cols] = (qkv[:, 0:128] + brow[:, 0:128]).astype(BF) * jnp.asarray(0.125, BF)
        k_o[:, cols] = qkv[:, 128:256].astype(BF)
        v_o[:, cols] = (qkv[:, 256:384] + brow[:, 256:384]).astype(BF)

    def slot(s, _):
        rows = pl.ds(pl.multiple_of(s * SLOT, SLOT), SLOT)
        place = scal[3] + s
        mask = slot_bias(lens[2 * place], lens[2 * place + 1])
        for c in range(2):
            cols = slice(c * 128, (c + 1) * 128)
            st = dot_nt(k_o[rows, cols], head_stack(q_o[rows, cols])) + mask
            top = jnp.maximum(jnp.max(st, 0, keepdims=True), -1e29)
            e = jnp.exp(st - top)
            den = jnp.sum(e, 0, keepdims=True)
            pt = (e * (1.0 / jnp.where(den == 0.0, 1.0, den))).astype(BF)
            pt_o[rows, c * 256 : (c + 1) * 256] = pt
            att_o[rows, cols] = dot(untranspose(pt), head_stack(v_o[rows, cols])).astype(BF)
        return 0

    lax.fori_loop(0, slots, slot, 0, unroll=SLOT_UNROLL)
    hid = base[...]
    for c, w in enumerate((wa, wb)):
        wo = jnp.concatenate([w[b * 128 : (b + 1) * 128, 384:512] for b in range(4)], 1)
        hid += dot(att_o[:, c * 128 : (c + 1) * 128], wo)
    hid_o[...] = hid
    if last:

        def tile(m, _):
            here = pl.ds(pl.multiple_of(m * BR, BR), BR)
            xhat, _ = normalise(hid_o[here, :])
            n2 = (xhat * gain[...] + bias[...]).astype(BF)
            n2_o[here, :] = n2
            n2t_o[:, here] = n2.T
            return 0

        lax.fori_loop(0, n1.shape[0] // BR, tile, 0)


def gelu_pair(u):
    phi = 0.5 + 0.5 * lax.erf(u * 0.7071067811865476)
    return u * phi, phi + u * (jnp.exp(-0.5 * (u * u)) * 0.3989422804014327)


def mlp_kernel(first, *refs):
    if first:
        (n2, n2t, cot, cott, ba, bb, ua, ub, da, db, gua, gub, gda, gdb, out, dn2, act_s, gup_s) = refs
    else:
        (n2, n2t, cot, cott, ba, bb, ua, ub, da, db, out_i, dn2_i, gua, gub, gda, gdb, out, dn2, act_s, gup_s) = refs
    bias = [b[D : D + BIAS, :].astype(F32)[1:2] for b in (ba, bb)]

    def tile(m, sums):
        here = pl.ds(pl.multiple_of(m * BR, BR), BR)
        n, c = n2[here, :], cot[here, :]
        new, acts, gups = [], [], []
        for j, (u, d) in enumerate(((ua, da), (ub, db))):
            up = dot(n, u[...]) + bias[j]
            dact = dot_nt(c, d[...])
            act, slope = gelu_pair(up)
            gup = (slope * dact).astype(BF)
            act = act.astype(BF)
            act_s[here, j * D : (j + 1) * D] = act
            gup_s[here, j * D : (j + 1) * D] = gup
            new.append(sums[j] + jnp.sum(gup.astype(F32), 0, keepdims=True))
            acts.append(act)
            gups.append(gup)
        o = dot(acts[0], da[...]) + dot(acts[1], db[...])
        e = dot_nt(gups[0], ua[...]) + dot_nt(gups[1], ub[...])
        out[here, :] = o if first else out_i[here, :] + o
        dn2[here, :] = e if first else dn2_i[here, :] + e
        return tuple(new)

    zero = jnp.zeros((1, D), F32)
    sums = lax.fori_loop(0, n2.shape[0] // BR, tile, (zero, zero), unroll=True)
    row = lax.broadcasted_iota(jnp.int32, (BIAS, D), 0)
    for j, (gu_o, gd_o) in enumerate(((gua, gda), (gub, gdb))):
        cols = slice(j * D, (j + 1) * D)
        gu_o[0:D, :] = dot(n2t[...], gup_s[:, cols]).astype(BF)
        gd_o[0:D, :] = dot(cott[...], act_s[:, cols]).astype(BF)
        high = sums[j].astype(BF).astype(F32)
        gu_o[D : D + BIAS, :] = jnp.where(row == 0, high, jnp.where(row == 8, sums[j] - high, 0.0)).astype(BF)


def attn_bwd_kernel(*refs):
    (x, hid, mlp, dn2, cot, g1, g2, bdown) = refs[:8]
    (q0, k0, v0, att0, pt0, q1, k1, v1, att1, pt1) = refs[8:18]
    w = refs[18:22]
    n1t = refs[22]
    block_o, gin_o = refs[23:25]
    ga = refs[25:29]
    (dq_s, dk_s, dv_s, dh_s, gat_s, gatt_s, datt_s) = refs[29:]
    rows_all = x.shape[0]

    def total(sums, *adds):
        return sums + jnp.concatenate([jnp.sum(a, 0, keepdims=True) for a in adds], 0)

    def ln2_back(m, sums):
        here = pl.ds(pl.multiple_of(m * BR, BR), BR)
        hidden = hid[here, :]
        block_o[here, :] = (hidden + mlp[here, :] + bdown[...].astype(F32)).astype(BF)
        xhat2, rstd2 = normalise(hidden)
        dn = dn2[here, :]
        e = dn * g2[...]
        cotf = cot[here, :].astype(F32)
        dh = cotf + rstd2 * (e - jnp.mean(e, -1, keepdims=True) - xhat2 * jnp.mean(e * xhat2, -1, keepdims=True))
        dh_s[here, :] = dh
        gat = dh.astype(BF)
        gat_s[here, :] = gat
        gatt_s[:, here] = gat.T
        return total(sums, gat.astype(F32), dn * xhat2, dn, cotf)

    sums2 = lax.fori_loop(0, rows_all // BR, ln2_back, jnp.zeros((4, D), F32))
    for c in range(4):
        wo = jnp.concatenate([w[c][b * 128 : (b + 1) * 128, 384:512] for b in range(4)], 1)
        datt_s[:, c * 128 : (c + 1) * 128] = dot_nt(gat_s[...], wo).astype(BF)

    def slot(s, _):
        rows = pl.ds(pl.multiple_of(s * SLOT, SLOT), SLOT)
        for c in range(4):
            q, k, v, pt_r = ((q0, k0, v0, pt0), (q1, k1, v1, pt1))[c // 2]
            cols = slice((c % 2) * 128, (c % 2 + 1) * 128)
            out = slice(c * 128, (c + 1) * 128)
            qs = head_stack(q[rows, cols])
            ks = head_stack(k[rows, cols])
            das = head_stack(datt_s[rows, out])
            pt = pt_r[rows, (c % 2) * 256 : (c % 2 + 1) * 256]
            dpt = dot_nt(v[rows, cols], das)
            ptf = pt.astype(F32)
            delta = jnp.sum(ptf * dpt, 0, keepdims=True)
            ds = (ptf * (dpt - delta)).astype(BF)
            dv_s[rows, out] = dot(pt, das).astype(BF)
            dk_s[rows, out] = dot(ds, qs).astype(BF)
            dq_s[rows, out] = (dot(untranspose(ds), ks) * 0.125).astype(BF)
        return 0

    lax.fori_loop(0, rows_all // SLOT, slot, 0, unroll=SLOT_UNROLL)

    def ln1_back(m, sums):
        here = pl.ds(pl.multiple_of(m * BR, BR), BR)
        dn1 = None
        for c in range(4):
            cols = slice(c * 128, (c + 1) * 128)
            grads = jnp.concatenate([dq_s[here, cols], dk_s[here, cols], dv_s[here, cols]], 1)
            part = dot_nt(grads, w[c][0:D, 0:384])
            dn1 = part if dn1 is None else dn1 + part
        xhat1, rstd1 = normalise(x[here, :].astype(F32))
        e = dn1 * g1[...]
        back = rstd1 * (e - jnp.mean(e, -1, keepdims=True) - xhat1 * jnp.mean(e * xhat1, -1, keepdims=True))
        gin_o[here, :] = (dh_s[here, :] + back).astype(BF)
        return total(sums, dn1 * xhat1, dn1, dq_s[here, :].astype(F32), dv_s[here, :].astype(F32))

    sums1 = lax.fori_loop(0, rows_all // BR, ln1_back, jnp.zeros((4, D), F32), unroll=True)
    zero = jnp.zeros((1, 128), F32)
    for j, s in enumerate((dq_s, dk_s, dv_s)):
        g = dot(n1t[...], s[...]).astype(BF)
        for c in range(4):
            ga[c][0:D, j * 128 : (j + 1) * 128] = g[:, c * 128 : (c + 1) * 128]
    go = [dot(gatt_s[...], a[...]).astype(BF) for a in (att0, att1)]
    for c in range(4):
        cols = slice(c * 128, (c + 1) * 128)
        ga[c][0:D, 384:512] = go[c // 2][:, (c % 2) * 128 : (c % 2 + 1) * 128]
        own = jnp.concatenate([sums1[2:3, cols], zero, sums1[3:4, cols], zero], 1)
        block = jnp.concatenate([own, sums1[0:2], sums2, jnp.zeros((1, D), F32)], 0)
        high = block.astype(BF)
        ga[c][D : D + 8, :] = high
        ga[c][D + 8 : D + 16, :] = (block - high.astype(F32)).astype(BF)


def bias_sum(refs, n):
    total = None
    for r in refs:
        v = r[n : n + BIAS, :].astype(F32)
        v = v[0:8] + v[8:16]
        total = v if total is None else total + v
    return total


def bias_block(total):
    high = total.astype(BF)
    return jnp.concatenate([high, (total - high.astype(F32)).astype(BF)], 0)


def combine_kernel(n_in, split, biased, last, *refs):
    scal = refs[0]
    ins, outs = refs[1 : 1 + n_in], refs[1 + n_in :]
    n = ins[0].shape[0] - (BIAS if biased else 0)

    def summed(rows):
        total = ins[0][rows, :].astype(F32)
        for r in ins[1:]:
            total += r[rows, :].astype(F32)
        return total.astype(BF)

    if split is None:
        outs[0][0:n, :] = summed(slice(0, n))
    else:
        bit = scal[split]
        h = n // 2
        outs[0][0:h, :] = summed(pl.ds(pl.multiple_of((1 - bit) * h, h), h))
        outs[1][0:h, :] = summed(pl.ds(pl.multiple_of(bit * h, h), h))
    if biased:
        total = bias_sum(ins, n)
        if last:
            outs[-1][...] = total
        else:
            block = bias_block(total)
            for o in outs:
                o[o.shape[0] - BIAS :, :] = block


def combine(scal, ins, split=None, biased=False, last=False):
    n = ins[0].shape[0] - (BIAS if biased else 0)
    extra = BIAS if biased and not last else 0
    if split is None:
        shapes = [sds((n + extra, D))]
    else:
        shapes = [sds((n // 2 + extra, D))] * 2
    if biased and last:
        shapes.append(sds((8, D), F32))
    return pl.pallas_call(
        functools.partial(combine_kernel, len(ins), split, biased, last),
        out_shape=shapes,
        in_specs=[SMEM()] + [VMEM()] * len(ins),
        out_specs=[VMEM()] * len(shapes),
        compiler_params=params(16),
        cost_estimate=cost(n * D * len(ins), 2 * n * D * (len(ins) + 1)),
        name="combine",
    )(scal, *ins)


def join_kernel(bit_at, scal, mine, other, out):
    bit = scal[bit_at]
    h = mine.shape[0]
    out[pl.ds(pl.multiple_of(bit * h, h), h), :] = mine[...]
    out[pl.ds(pl.multiple_of((1 - bit) * h, h), h), :] = other[...]


def join(scal, mine, other, bit_at):
    h = mine.shape[0]
    return pl.pallas_call(
        functools.partial(join_kernel, bit_at),
        out_shape=sds((2 * h, D)),
        in_specs=[SMEM(), VMEM(), VMEM()],
        out_specs=VMEM(),
        compiler_params=params(16),
        cost_estimate=cost(h, 8 * h * D),
        name="join",
    )(scal, mine, other)


def final_kernel(kind, bit_at, scal, mine, other, *outs):
    bit = scal[bit_at]
    h = mine.shape[0]
    for place, ref in ((bit, mine), (1 - bit, other)):
        at = pl.ds(pl.multiple_of(place * h, h), h)
        v = ref[...].astype(F32)
        if kind == "up":
            outs[0][at, :] = v
        elif kind == "down":
            outs[0][:, at] = v.T
        else:
            for j in range(3):
                outs[j][at, :] = v[:, j * 128 : (j + 1) * 128]
            outs[3][:, at] = v[:, 384:512].T


def final(scal, kind, mine, other, bit_at):
    if kind == "attn":
        shapes = [sds((D, 128), F32)] * 3 + [sds((128, D), F32)]
    else:
        shapes = [sds((D, D), F32)]
    return pl.pallas_call(
        functools.partial(final_kernel, kind, bit_at),
        out_shape=shapes,
        in_specs=[SMEM(), VMEM(), VMEM()],
        out_specs=[VMEM()] * len(shapes),
        compiler_params=params(16),
        cost_estimate=cost(D * D, 6 * D * D),
        name="final_" + kind,
    )(scal, mine, other)


def layer(
    n_dp, n_t, x, lengths, ln1_gain, ln1_bias, w_query, b_query, w_key, w_value, b_value, w_out, b_out,
    ln2_gain, ln2_bias, w_up, b_up, w_down, b_down, cot,
):
    rows = x.shape[0]
    dp_at, t_at = lax.axis_index("dp"), lax.axis_index("tensor")
    slots = rows // SLOT
    scal = jnp.stack([dp_at & 1, (dp_at >> 1) & 1, t_at, t_at * slots]).astype(jnp.int32)
    lens = lengths.reshape(-1)

    def swap(v, dp_mask=0, t_mask=0):
        pairs = [(d * n_t + t, (d ^ dp_mask) * n_t + (t ^ t_mask)) for d in range(n_dp) for t in range(n_t)]
        return lax.ppermute(v, ("dp", "tensor"), pairs)

    row = lambda v: v.reshape(1, -1)
    wa = [None] * 4
    wa[0] = pl.pallas_call(
        pack_kernel, out_shape=sds((D + BIAS, D)), in_specs=[VMEM()] * 7, out_specs=VMEM(),
        compiler_params=params(16), cost_estimate=cost(D, 4 * D * D), name="pack",
    )(w_query, w_key, w_value, w_out, row(b_query), row(b_value), row(b_up))
    wu, wd = [w_up, None, None, None], [w_down, None, None, None]
    wa[2] = swap(wa[0], t_mask=2)
    wa[1] = swap(wa[0], t_mask=1)
    wu[1] = swap(wu[0], t_mask=1)
    wd[1] = swap(wd[0], t_mask=1)
    wu[2] = swap(wu[0], t_mask=2)
    wd[2] = swap(wd[0], t_mask=2)
    wa[3] = swap(wa[2], t_mask=1)
    wu[3] = swap(wu[2], t_mask=1)
    wd[3] = swap(wd[2], t_mask=1)

    def call(kernel, name, out_shape, args, scratch=(), mib=16, flops=1e9, nbytes=1e7):
        return pl.pallas_call(
            kernel,
            out_shape=out_shape,
            in_specs=[SMEM() if a.dtype == jnp.int32 else VMEM() for a in args],
            out_specs=[VMEM()] * len(out_shape),
            scratch_shapes=list(scratch),
            compiler_params=params(mib),
            cost_estimate=cost(flops, nbytes),
            name=name,
        )(*args)

    wide, tall = sds((rows, D)), sds((D, rows))
    acc = sds((rows, D), F32)
    n1, n1t, cott, base = call(
        prep_kernel, "prep", [wide, tall, tall, acc], [x, row(ln1_gain), row(ln1_bias), row(b_out), cot]
    )
    saved = [sds((rows, 256))] * 4 + [sds((rows, 512)), acc]
    q0, k0, v0, att0, pt0, base = call(
        functools.partial(attn_fwd_kernel, False), "attn_fwd_own", saved, [scal, lens, n1, base, wa[0], wa[1]]
    )
    q1, k1, v1, att1, pt1, hid, n2, n2t = call(
        functools.partial(attn_fwd_kernel, True), "attn_fwd_other", saved + [wide, tall],
        [scal, lens, n1, base, wa[2], wa[3], row(ln2_gain), row(ln2_bias)],
    )

    def mlp(ia, ib, sums):
        return call(
            functools.partial(mlp_kernel, not sums), "mlp_other" if sums else "mlp_own",
            [sds((D + BIAS, D))] * 2 + [sds((D, D))] * 2 + [acc] * 2,
            [n2, n2t, cot, cott, wa[ia], wa[ib], wu[ia], wu[ib], wd[ia], wd[ib], *sums],
            [pltpu.VMEM((rows, 2 * D), BF)] * 2,
        )

    gu, gd, ga = [None] * 4, [None] * 4, [None] * 4
    gu[1], gu[0], gd[1], gd[0], out_a, dn2_a = mlp(1, 0, ())
    gu[3], gu[2], gd[3], gd[2], out_sum, dn2 = mlp(3, 2, (out_a, dn2_a))
    half = pltpu.VMEM((rows, D), BF)
    block_out, grad_in, *ga = call(
        attn_bwd_kernel, "attn_bwd", [wide] * 2 + [sds((D + BIAS, D))] * 4,
        [x, hid, out_sum, dn2, cot, row(ln1_gain), row(ln2_gain), row(b_down),
         q0, k0, v0, att0, pt0, q1, k1, v1, att1, pt1, *wa, n1t],
        [half] * 3 + [pltpu.VMEM((rows, D), F32), half, pltpu.VMEM((D, rows), BF), half],
        mib=24,
    )

    def reduce(g, kind, biased):
        got1, got3 = swap(g[1], t_mask=1), swap(g[3], t_mask=1)
        (for_y,) = combine(scal, [g[2], got3], biased=biased)
        from_y = swap(for_y, t_mask=2)
        send, keep = combine(scal, [g[0], got1, from_y], split=0, biased=biased)
        got = swap(send, dp_mask=1)
        send, keep = combine(scal, [keep, got], split=1, biased=biased)
        got = swap(send, dp_mask=2)
        parts, bit = [keep, got], 4
        while bit < n_dp:
            (total,) = combine(scal, parts, biased=biased)
            parts, bit = [total, swap(total, dp_mask=bit)], 2 * bit
        total, *sums = combine(scal, parts, biased=biased, last=True)
        quarter = join(scal, total, swap(total, dp_mask=2), 1)
        other = swap(quarter, dp_mask=1)
        return final(scal, kind, quarter, other, 0), sums

    (grad_w_down,), _ = reduce(gd, "down", False)
    (grad_w_up,), (sums_up,) = reduce(gu, "up", True)
    (gwq, gwk, gwv, gwo), (sums,) = reduce(ga, "attn", True)
    return (
        block_out, grad_in, sums[1], sums[2], gwq, sums[0, 0:128], gwk, gwv, sums[0, 256:384], gwo, sums[3],
        sums[4], sums[5], grad_w_up, sums_up[0], grad_w_down, sums[6],
    )


def solution(mesh):
    n_dp, n_t = mesh.shape["dp"], mesh.shape["tensor"]
    rows, cols, split, copied = P(("dp", "tensor"), None), P(None, "tensor"), P("tensor"), P()
    down = P("tensor", None)
    return jax.shard_map(
        functools.partial(layer, n_dp, n_t),
        mesh=mesh,
        in_specs=(
            rows, P("dp", None, None), copied, copied, cols, split, cols, cols, split, down, copied, copied, copied,
            cols, split, down, copied, rows,
        ),
        out_specs=(
            rows, rows, copied, copied, cols, split, cols, cols, split, down, copied, copied, copied, cols, split, down,
            copied,
        ),
        check_vma=False,
    )
```

```python
import functools

import jax
import jax.numpy as jnp
from jax import lax
from jax.experimental import pallas as pl
from jax.experimental.pallas import tpu as pltpu
from jax.sharding import PartitionSpec as P

BF, F32 = jnp.bfloat16, jnp.float32
D = 512
HD = 64
SLOT = 128
BR = 256
BIAS = 16
EPS = 1e-5
WEIGHTS = {"attn_dw_sent": 1, "attn_core_bwd": 1, "attn_dx": 1, "add_d_x": 0, "add_l_y": 0, "add_h_x": 0, "add_u_y": 0}
LN1_G, LN1_B, B_OUT, LN2_G, LN2_B, B_DOWN, B_UP, B_QV = range(8)
SMEM = functools.partial(pl.BlockSpec, memory_space=pltpu.SMEM)
VMEM = functools.partial(pl.BlockSpec, memory_space=pltpu.VMEM)


def dot(a, b):
    return lax.dot_general(a, b, (((1,), (0,)), ((), ())), preferred_element_type=F32)


def dot_nt(a, b):
    return lax.dot_general(a, b, (((1,), (1,)), ((), ())), preferred_element_type=F32)


def dot_tn(a, b):
    return lax.dot_general(a, b, (((0,), (0,)), ((), ())), preferred_element_type=F32)


def params(mib, **kw):
    return pltpu.CompilerParams(vmem_limit_bytes=mib << 20, **kw)


def cost(flops, nbytes, trans=0):
    return pl.CostEstimate(flops=int(flops), bytes_accessed=int(nbytes), transcendentals=int(trans))


def sds(shape, dtype=BF):
    return jax.ShapeDtypeStruct(shape, dtype)


def whole(shape):
    return pl.BlockSpec(shape, lambda *i: (0,) * len(shape))


def normalise(v):
    mean = jnp.mean(v, -1, keepdims=True)
    centred = v - mean
    rstd = lax.rsqrt(jnp.mean(centred * centred, -1, keepdims=True) + EPS)
    return centred * rstd, rstd


def head_stack(v):
    first = lax.broadcasted_iota(jnp.int32, v.shape, 1) < HD
    zero = jnp.zeros_like(v)
    return jnp.concatenate([jnp.where(first, v, zero), jnp.where(first, zero, v)], 0)


def untranspose(v):
    return jnp.concatenate([v[:, :SLOT].T, v[:, SLOT:].T], 1)


def slot_bias(len1, len2):
    def places(shape, dim):
        p = lax.broadcasted_iota(jnp.int32, shape, dim) & (SLOT - 1)
        second = (p >= SLOT // 2) & (len2 > 0)
        local = jnp.where(second, p - SLOT // 2, p)
        valid = local < jnp.where(second, len2, len1)
        base = jnp.where(second, 1000, 0)
        return valid, base, base + ((local * 43) >> 8)

    valid_k, _, frame_k = places((SLOT, 1), 0)
    valid_q, base_q, frame_q = places((1, 2 * SLOT), 1)
    frame_k = jnp.where(valid_k, frame_k, 1 << 20)
    frame_q = jnp.where(valid_q, frame_q, -1)
    allowed = (frame_k <= frame_q) & (frame_k >= base_q)
    return jnp.where(allowed, 0.0, -1e30).astype(F32)


def pack_kernel(*refs):
    wq, wk, wv, wo = refs[:4]
    small, (out, vecs), held, sems = refs[4:13], refs[13:15], refs[15:24], refs[24]
    copies = [pltpu.make_async_copy(v, h, sems.at[7 + i]) for i, (v, h) in enumerate(zip(small, held))]
    for i, ref in enumerate((wq, wk, wv)):
        copies.append(pltpu.make_async_copy(ref, out.at[0:D, i * 128 : (i + 1) * 128], sems.at[i]))
    for b in range(4):
        blk = slice(b * 128, (b + 1) * 128)
        copies.append(pltpu.make_async_copy(wo.at[:, blk], out.at[blk, 384:512], sems.at[3 + b]))
    for c in copies:
        c.start()
    for c in copies[: len(small)]:
        c.wait()
    rows = [h[...].astype(F32).reshape(1, h.shape[0]) for h in held]
    gap = jnp.zeros((1, 128), F32)
    rows[7:] = [jnp.concatenate([rows[7], gap, rows[8], gap], 1)]
    table = jnp.concatenate(rows, 0)
    vecs[...] = table
    row = lax.broadcasted_iota(jnp.int32, (BIAS, D), 0)
    block = jnp.where(row == 0, table[B_QV : B_QV + 1], jnp.where(row == 1, table[B_UP : B_UP + 1], 0.0))
    out[D : D + BIAS, :] = block.astype(BF)
    for c in copies[len(small) :]:
        c.wait()


def prep_kernel(x, vecs, n1_o):
    def tile(m, _):
        here = pl.ds(pl.multiple_of(m * BR, BR), BR)
        xhat, _ = normalise(x[here, :].astype(F32))
        n1_o[here, :] = (xhat * vecs[LN1_G : LN1_G + 1, :] + vecs[LN1_B : LN1_B + 1, :]).astype(BF)
        return 0

    lax.fori_loop(0, x.shape[0] // BR, tile, 0, unroll=2)


def attn_fwd_kernel(shares, first, last, *refs):
    (scal, lens, n1, base), w = refs[:4], refs[4 : 4 + shares]
    vecs, (q_o, k_o, v_o, att_o, pt_o, hid_o), n2_o = refs[4 + shares], refs[5 + shares : 11 + shares], refs[-1]
    slots = n1.shape[0] // SLOT

    for c in range(shares):
        brow = w[c][D : D + BIAS, :].astype(F32)[0:1]
        cols = slice(c * 128, (c + 1) * 128)
        qkv = dot(n1[...], w[c][0:D, 0:384])
        q_o[:, cols] = (qkv[:, 0:128] + brow[:, 0:128]).astype(BF) * jnp.asarray(0.125, BF)
        k_o[:, cols] = qkv[:, 128:256].astype(BF)
        v_o[:, cols] = (qkv[:, 256:384] + brow[:, 256:384]).astype(BF)

    def slot(s, _):
        rows = pl.ds(pl.multiple_of(s * SLOT, SLOT), SLOT)
        place = scal[3] + s
        mask = slot_bias(lens[0, place, 0], lens[0, place, 1])
        for c in range(shares):
            cols = slice(c * 128, (c + 1) * 128)
            st = dot_nt(k_o[rows, cols], head_stack(q_o[rows, cols])) + mask
            top = jnp.maximum(jnp.max(st, 0, keepdims=True), -1e29)
            e = jnp.exp(st - top)
            den = jnp.sum(e, 0, keepdims=True)
            pt = (e * (1.0 / jnp.where(den == 0.0, 1.0, den))).astype(BF)
            pt_o[rows, c * 256 : (c + 1) * 256] = pt
            att_o[rows, cols] = dot(untranspose(pt), head_stack(v_o[rows, cols])).astype(BF)
        return 0

    lax.fori_loop(0, slots, slot, 0, unroll=True)
    hid = base[...].astype(F32)
    if first:
        hid += vecs[B_OUT : B_OUT + 1, :]
    for c in range(shares):
        wo = jnp.concatenate([w[c][b * 128 : (b + 1) * 128, 384:512] for b in range(4)], 1)
        hid += dot(att_o[:, c * 128 : (c + 1) * 128], wo)
    hid_o[...] = hid
    if last:

        def tile(m, _):
            here = pl.ds(pl.multiple_of(m * BR, BR), BR)
            xhat, _ = normalise(hid_o[here, :])
            n2_o[here, :] = (xhat * vecs[LN2_G : LN2_G + 1, :] + vecs[LN2_B : LN2_B + 1, :]).astype(BF)
            return 0

        lax.fori_loop(0, n1.shape[0] // BR, tile, 0, unroll=2)


def gelu_pair(u):
    phi = 0.5 + 0.5 * lax.erf(u * 0.7071067811865476)
    return u * phi, phi + u * (jnp.exp(-0.5 * (u * u)) * 0.3989422804014327)


def mlp_kernel(first, *refs):
    if first:
        (n2, cot, ba, bb, ua, ub, da, db, gua, gub, gda, gdb, out, dn2, act_s, gup_s) = refs
    else:
        (n2, cot, ba, bb, ua, ub, da, db, out_i, dn2_i, gua, gub, gda, gdb, out, dn2, act_s, gup_s) = refs
    bias = [b[D : D + BIAS, :].astype(F32)[1:2] for b in (ba, bb)]

    def tile(m, sums):
        here = pl.ds(pl.multiple_of(m * BR, BR), BR)
        n, c = n2[here, :], cot[here, :]
        new, acts, gups = [], [], []
        for j, (u, d) in enumerate(((ua, da), (ub, db))):
            up = dot(n, u[...]) + bias[j]
            dact = dot_nt(c, d[...])
            act, slope = gelu_pair(up)
            gup = (slope * dact).astype(BF)
            act = act.astype(BF)
            act_s[here, j * D : (j + 1) * D] = act
            gup_s[here, j * D : (j + 1) * D] = gup
            new.append(sums[j] + jnp.sum(gup.astype(F32), 0, keepdims=True))
            acts.append(act)
            gups.append(gup)
        o = dot(acts[0], da[...]) + dot(acts[1], db[...])
        e = dot_nt(gups[0], ua[...]) + dot_nt(gups[1], ub[...])
        out[here, :] = o if first else out_i[here, :] + o
        dn2[here, :] = e if first else dn2_i[here, :] + e
        return tuple(new)

    zero = jnp.zeros((1, D), F32)
    sums = lax.fori_loop(0, n2.shape[0] // BR, tile, (zero, zero), unroll=True)
    row = lax.broadcasted_iota(jnp.int32, (BIAS, D), 0)
    for j, (gu_o, gd_o) in enumerate(((gua, gda), (gub, gdb))):
        cols = slice(j * D, (j + 1) * D)
        gu_o[0:D, :] = dot_tn(n2[...], gup_s[:, cols]).astype(BF)
        gd_o[0:D, :] = dot_tn(cot[...], act_s[:, cols]).astype(BF)
        high = sums[j].astype(BF).astype(F32)
        gu_o[D : D + BIAS, :] = jnp.where(row == 0, high, jnp.where(row == 8, sums[j] - high, 0.0)).astype(BF)


def act_kernel(n2, cot, bias, u, act_o, slope_o, gd_o):
    add = bias[D : D + BIAS, :].astype(F32)[1:2]

    def tile(m, _):
        here = pl.ds(pl.multiple_of(m * BR, BR), BR)
        act, slope = gelu_pair(dot(n2[here, :], u[...]) + add)
        act_o[here, :] = act.astype(BF)
        slope_o[here, :] = slope
        return 0

    lax.fori_loop(0, n2.shape[0] // BR, tile, 0, unroll=True)
    gd_o[...] = dot_tn(cot[...], act_o[...]).astype(BF)


def down_kernel(n2, cot, act, slope, u, d, out_i, dn2_i, gu_o, out, dn2, gup_s):
    def tile(m, sums):
        here = pl.ds(pl.multiple_of(m * BR, BR), BR)
        gup = (slope[here, :] * dot_nt(cot[here, :], d[...])).astype(BF)
        gup_s[here, :] = gup
        out[here, :] = out_i[here, :] + dot(act[here, :], d[...])
        dn2[here, :] = dn2_i[here, :] + dot_nt(gup, u[...])
        return sums + jnp.sum(gup.astype(F32), 0, keepdims=True)

    sums = lax.fori_loop(0, n2.shape[0] // BR, tile, jnp.zeros((1, D), F32), unroll=True)
    gu_o[0:D, :] = dot_tn(n2[...], gup_s[...]).astype(BF)
    gu_o[D : D + BIAS, :] = bias_block(jnp.concatenate([sums, jnp.zeros((7, D), F32)], 0))


def total(sums, *adds):
    return sums + jnp.concatenate([jnp.sum(a, 0, keepdims=True) for a in adds], 0)


def ln2_bwd_kernel(hid, mlp, dn2, cot, vecs, *refs):
    w, (block_o, dh_o, gat_s, datt_o, sums_o) = refs[:4], refs[4:]
    rows = hid.shape[0]

    def tile(m, sums):
        here = pl.ds(pl.multiple_of(m * BR, BR), BR)
        hidden = hid[here, :]
        block_o[here, :] = (hidden + mlp[here, :] + vecs[B_DOWN : B_DOWN + 1, :]).astype(BF)
        xhat, rstd = normalise(hidden)
        dn = dn2[here, :]
        e = dn * vecs[LN2_G : LN2_G + 1, :]
        cotf = cot[here, :].astype(F32)
        dh = cotf + rstd * (e - jnp.mean(e, -1, keepdims=True) - xhat * jnp.mean(e * xhat, -1, keepdims=True))
        dh_o[here, :] = dh
        gat = dh.astype(BF)
        gat_s[here, :] = gat
        return total(sums, gat.astype(F32), dn * xhat, dn, cotf)

    sums_o[0:4, :] = lax.fori_loop(0, rows // BR, tile, jnp.zeros((4, D), F32), unroll=2)
    sums_o[4:8, :] = jnp.zeros((4, D), F32)
    for c in range(4):
        wo = jnp.concatenate([w[c][b * 128 : (b + 1) * 128, 384:512] for b in range(4)], 1)
        datt_o[:, c * 128 : (c + 1) * 128] = dot_nt(gat_s[...], wo).astype(BF)


def attn_core_bwd_kernel(*refs):
    saved, (datt, dq_o, dk_o, dv_o) = refs[:12], refs[12:]
    where = ((0, 0), (0, 1), (1, 0), (2, 0))

    def slot(s, _):
        rows = pl.ds(pl.multiple_of(s * SLOT, SLOT), SLOT)
        held = []
        for c, (group, at) in enumerate(where):
            q, k, v, pt_r = saved[4 * group : 4 * group + 4]
            cols = slice(at * 128, (at + 1) * 128)
            out = slice(c * 128, (c + 1) * 128)
            das = head_stack(datt[rows, out])
            pt = pt_r[rows, at * 256 : (at + 1) * 256]
            dpt = dot_nt(v[rows, cols], das)
            dv_o[rows, out] = dot(pt, das).astype(BF)
            held.append((q, k, cols, out, pt, dpt))
        ready = []
        for q, k, cols, out, pt, dpt in held:
            ptf = pt.astype(F32)
            delta = jnp.sum(ptf * dpt, 0, keepdims=True)
            ds = (ptf * (dpt - delta)).astype(BF)
            ready.append((q, k, cols, out, ds, untranspose(ds)))
        for q, k, cols, out, ds, dst in ready:
            dq_o[rows, out] = (dot(dst, head_stack(k[rows, cols])) * 0.125).astype(BF)
            dk_o[rows, out] = dot(ds, head_stack(q[rows, cols])).astype(BF)
        return 0

    lax.fori_loop(0, datt.shape[0] // SLOT, slot, 0, unroll=True)


def attn_dw_kernel(one, two, dq, dk, dv, n1, gat, shared, att_one, att_two, *ga):
    gap, rest = jnp.zeros((1, 128), F32), shared[0:7, :]
    grads = [[s[:, c * 128 : (c + 1) * 128] for s in (dq, dk, dv)] for c in (one, two)]
    sums = [[jnp.sum(g[j].astype(F32), 0, keepdims=True) for j in (0, 2)] for g in grads]
    g = dot_tn(n1[...], jnp.concatenate(grads[0] + grads[1], 1)).astype(BF)
    att = [a[...] if a.shape[1] == 128 else a[:, (c % 2) * 128 : (c % 2 + 1) * 128] for a, c in zip((att_one, att_two), (one, two))]
    go = dot_tn(gat[...], jnp.concatenate(att, 1)).astype(BF)
    for i in range(2):
        o, at = ga[i % len(ga)], 0 if len(ga) == 2 else i * (D + BIAS)
        o[at : at + D, 0:384] = g[:, i * 384 : (i + 1) * 384]
        o[at : at + D, 384:512] = go[:, i * 128 : (i + 1) * 128]
        own = jnp.concatenate([sums[i][0], gap, sums[i][1], gap], 1)
        o[at + D : at + D + BIAS, :] = bias_block(jnp.concatenate([own, rest], 0))


def attn_dx_kernel(x, dh, dq, dk, dv, sums2, vecs, *refs):
    w, (gin_o, shared_o) = refs[:4], refs[4:]

    def tile(m, sums):
        here = pl.ds(pl.multiple_of(m * BR, BR), BR)
        dn1 = None
        for c in range(4):
            cols = slice(c * 128, (c + 1) * 128)
            grads = jnp.concatenate([dq[here, cols], dk[here, cols], dv[here, cols]], 1)
            part = dot_nt(grads, w[c][0:D, 0:384])
            dn1 = part if dn1 is None else dn1 + part
        xhat, rstd = normalise(x[here, :].astype(F32))
        e = dn1 * vecs[LN1_G : LN1_G + 1, :]
        back = rstd * (e - jnp.mean(e, -1, keepdims=True) - xhat * jnp.mean(e * xhat, -1, keepdims=True))
        gin_o[here, :] = (dh[here, :] + back).astype(BF)
        return total(sums, dn1 * xhat, dn1)

    sums1 = lax.fori_loop(0, x.shape[0] // BR, tile, jnp.zeros((2, D), F32), unroll=True)
    shared_o[...] = jnp.concatenate([sums1, sums2[0:4, :], jnp.zeros((2, D), F32)], 0)


def bias_block(total):
    high = total.astype(BF)
    return jnp.concatenate([high, (total - high.astype(F32)).astype(BF)], 0)


class Part:
    def __init__(self, n, sources, sums=()):
        self.n, self.sources, self.sums = n, sources, sums
        self.extra = BIAS if sums else 0


def combine_kernel(parts, op, *refs):
    scal, ins = refs[0], refs[1:]
    n_in = 1 + max(i for part in parts for i, _ in part[1] + part[2])
    ins, outs = ins[:n_in], ins[n_in:]

    def summed(part, start, size):
        acc = None
        for i, first in part[1]:
            v = ins[i][pl.ds(first + start, size), :].astype(F32)
            acc = v if acc is None else acc + v
        return acc.astype(BF)

    def sums(part):
        rows = [ins[i][first : first + BIAS, :].astype(F32) for i, first in part[2]]
        terms = [v[0:8] + v[8:16] for v in rows]
        while len(terms) > 1:
            terms = [sum(terms[i + 1 : i + 2], terms[i]) for i in range(0, len(terms), 2)]
        return terms[0]

    if op == "y":
        for o, part in zip(outs, (parts[1], parts[0])):
            n = part[0]
            o[0:n, :] = summed(part, 0, n)
            if part[2]:
                o[n : n + BIAS, :] = bias_block(sums(part))
        return
    at, side = 0, 1
    for part in parts:
        n, biased = part[0], bool(part[2])
        if op in ("all", "last"):
            outs[0][at : at + n, :] = summed(part, 0, n)
            at += n
            if biased and op == "last":
                outs[side][...] = sums(part)
                side += 1
            elif biased:
                outs[0][at : at + BIAS, :] = bias_block(sums(part))
                at += BIAS
        else:
            bit, h = scal[op], n // 2
            outs[0][at : at + h, :] = summed(part, pl.multiple_of((1 - bit) * h, h), h)
            outs[1][at : at + h, :] = summed(part, pl.multiple_of(bit * h, h), h)
            at += h
            if biased:
                block = bias_block(sums(part))
                for o in outs:
                    o[at : at + BIAS, :] = block
                at += BIAS


def join_kernel(scal, mine, other, out):
    bit, n = scal[1], mine.shape[0]
    out[pl.ds(pl.multiple_of(bit * n, n), n), :] = mine[...]
    out[pl.ds(pl.multiple_of((1 - bit) * n, n), n), :] = other[...]


def final_kernel(kind, *refs):
    scal, outs = refs[0], refs[-1:] if kind != "attn" else refs[-5:]
    got = refs[1 : len(refs) - len(outs)]
    x, z = scal[0], scal[1]
    if len(got) == 2:
        places = (x, 1 - x)
    else:
        places = (x * 2 + z, x * 2 + 1 - z, (1 - x) * 2 + z, (1 - x) * 2 + 1 - z)
    halves = 2 if kind == "attn" else 1
    n = got[0].shape[0] // halves
    for half in range(halves):
        for place, ref in zip(places, got):
            at = pl.ds(pl.multiple_of(half * 4 * n + place * n, n), n)
            v = ref[half * n : (half + 1) * n, :].astype(F32)
            if kind == "up":
                outs[0][at, :] = v
            elif kind == "down":
                outs[0][:, at] = v.T
            else:
                for j in range(3):
                    outs[j][at, :] = v[:, j * 128 : (j + 1) * 128]
                outs[4][at, :] = v[:, 384:512]
    if kind == "attn":
        outs[3][...] = outs[4][...].T


def layer(
    n_dp, n_t, x, lengths, ln1_gain, ln1_bias, w_query, b_query, w_key, w_value, b_value, w_out, b_out,
    ln2_gain, ln2_bias, w_up, b_up, w_down, b_down, cot,
):
    rows = x.shape[0]
    dp_at, t_at = lax.axis_index("dp"), lax.axis_index("tensor")
    scal = jnp.stack([dp_at & 1, (dp_at >> 1) & 1, t_at, t_at * (rows // SLOT)]).astype(jnp.int32)
    last = [scal]

    class Swap:
        def __init__(self, v, dp_mask=0, t_mask=0):
            self.v, self.masks, self.shape, self.made = v, (dp_mask, t_mask), v.shape, None

        def get(self):
            if self.made is None:
                self.made = swap_now(self.v, *self.masks)
            return self.made

    def real(v):
        return v.get() if isinstance(v, Swap) else v

    def swap(v, dp_mask=0, t_mask=0):
        return Swap(real(v), dp_mask, t_mask)

    def swap_now(v, dp_mask=0, t_mask=0):
        pairs = [(d * n_t + t, (d ^ dp_mask) * n_t + (t ^ t_mask)) for d in range(n_dp) for t in range(n_t)]
        return lax.ppermute(v, ("dp", "tensor"), pairs)

    def after(v, *tokens):
        return lax.optimization_barrier((real(v), *tokens))[0]

    def hbm(v):
        return pltpu.with_memory_space_constraint(v, pltpu.HBM)

    def call(kernel, name, out_shape, args, scratch=(), mib=16, in_hbm=False, weight=10):
        args = [real(a) for a in args]
        if last[0] is not scal:
            i = max(range(len(args)), key=lambda j: args[j].size)
            args[i] = after(args[i], last[0])
        specs = [SMEM() if a.dtype == jnp.int32 else VMEM() for a in args]
        if in_hbm:
            args = [hbm(a) for a in args]
            specs = [pl.BlockSpec(memory_space=pltpu.HBM)] * len(args)
        out = pl.pallas_call(
            kernel,
            out_shape=out_shape,
            in_specs=specs,
            out_specs=[VMEM()] * len(out_shape),
            scratch_shapes=list(scratch),
            compiler_params=params(mib),
            cost_estimate=cost(WEIGHTS.get(name, weight) * 10**9, 10**8),
            name=name,
        )(*args)
        last[0] = min(out, key=lambda o: o.size)
        return out

    def combine(op, *parts, tag="z"):
        arrays = []
        for part in parts:
            for array, _ in (*part.sources, *part.sums):
                array = real(array)
                if not any(array is known for known in arrays):
                    arrays.append(array)
        place = lambda array: next(i for i, known in enumerate(arrays) if known is real(array))
        spec = tuple((p.n, *(tuple((place(v), first) for v, first in w) for w in (p.sources, p.sums))) for p in parts)
        if op == "y":
            shapes = [sds((p.n + p.extra, D)) for p in (parts[1], parts[0])]
        elif op == "all":
            shapes = [sds((sum(p.n + p.extra for p in parts), D))]
        elif op == "last":
            shapes = [sds((sum(p.n for p in parts), D))] + [sds((8, D), F32) for p in parts if p.sums]
        else:
            shapes = [sds((sum(p.n // 2 + p.extra for p in parts), D))] * 2
        return call(functools.partial(combine_kernel, spec, op), "add_" + tag, shapes, [scal, *arrays], mib=8)

    own, vecs = call(
        pack_kernel, "pack", [sds((D + BIAS, D)), sds((8, D), F32)],
        [w_query, w_key, w_value, w_out, ln1_gain, ln1_bias, b_out, ln2_gain, ln2_bias, b_down, b_up, b_query, b_value],
        [pltpu.VMEM((D,), F32)] * 2 + [pltpu.VMEM((D,), BF)] + [pltpu.VMEM((D,), F32)] * 2 + [pltpu.VMEM((D,), BF)] * 2
        + [pltpu.VMEM((128,), BF)] * 2 + [pltpu.SemaphoreType.DMA((16,))],
        in_hbm=True,
    )
    wide, acc = sds((rows, D)), sds((rows, D), F32)
    wa_y, wa_c = swap(own, t_mask=2), swap(own, t_mask=1)
    (n1,) = call(prep_kernel, "prep", [wide], [x, vecs])
    wu_y = swap(after(w_up, n1), t_mask=2)
    wd_y = swap(after(w_down, n1), t_mask=2)

    def attn_fwd(name, weights, hid, first=False, last=False):
        n = 128 * len(weights)
        shapes = [sds((rows, n))] * 4 + [sds((rows, 2 * n)), acc] + [wide] * last
        args = [scal, lengths, n1, hid, *weights, vecs]
        return call(functools.partial(attn_fwd_kernel, len(weights), first, last), name, shapes, args)

    *saved_0, att0, pt0, hid = attn_fwd("attn_fwd_own", [own, wa_c], x, first=True)
    wa_y = after(wa_y, hid)
    wa_yc = swap(wa_y, t_mask=1)
    *saved_2, att2, pt2, hid = attn_fwd("attn_fwd_y", [wa_y], hid)
    wu_c, wd_c = swap(after(w_up, hid), t_mask=1), swap(after(w_down, hid), t_mask=1)
    *saved_3, att3, pt3, hid, n2 = attn_fwd("attn_fwd_yc", [wa_yc], hid, last=True)
    wa = [own, wa_c, wa_y, wa_yc]

    def part(n, *arrays, first=0, sums=True):
        return Part(n, [(v, first) for v in arrays], [(v, v.shape[0] - BIAS) for v in arrays] if sums else ())

    h, q = D // 2, D // 4
    bits = [1 << b for b in range(2, n_dp.bit_length() - 1)]
    gu1, gu0, gd1, gd0, out_sum, dn2 = call(
        functools.partial(mlp_kernel, True), "mlp_own", [sds((D + BIAS, D))] * 2 + [sds((D, D))] * 2 + [acc] * 2,
        [n2, cot, wa_c, own, wu_c, w_up, wd_c, w_down], [pltpu.VMEM((rows, 2 * D), BF)] * 2,
    )
    gd1, gu1 = swap(gd1, t_mask=1), swap(gu1, t_mask=1)
    wu_y = after(wu_y, out_sum)
    wu_yc = swap(wu_y, t_mask=1)

    def up(name, bias, u):
        return call(act_kernel, name, [wide, acc, sds((D, D))], [n2, cot, bias, u])

    def down(name, act, slope, u, d, *sums):
        return call(
            down_kernel, name, [sds((D + BIAS, D))] + [acc] * 2, [n2, cot, act, slope, u, d, *sums],
            [pltpu.VMEM((rows, D), BF)],
        )

    act2, slope2, gd2 = up("mlp_up_y", wa_y, wu_y)
    act3, slope3, gd3 = up("mlp_up_yc", wa_yc, wu_yc)
    gd3 = swap(gd3, t_mask=1)
    send, keep_u0 = combine(0, part(D, gu0, gu1), tag="u0")
    got_u0 = swap(send, dp_mask=1)
    send, keep_d = combine("y", part(D, gd0, gd1, sums=False), part(D, gd2, gd3, sums=False), tag="d_y")
    got_d = swap(send, t_mask=2)
    wd_y = after(wd_y, send)
    wd_yc = swap(wd_y, t_mask=1)
    gu2, out_sum, dn2 = down("mlp_down_y", act2, slope2, wu_y, wd_y, out_sum, dn2)
    gu3, out_sum, dn2 = down("mlp_down_yc", act3, slope3, wu_yc, wd_yc, out_sum, dn2)
    gu3 = swap(gu3, t_mask=1)
    block_out, dh, gat, datt, sums2 = call(
        ln2_bwd_kernel, "ln2_bwd", [wide, acc, wide, wide, sds((8, D), F32)], [hid, out_sum, dn2, cot, vecs, *wa]
    )
    send, keep_u2 = combine(0, part(D, gu2, gu3), tag="u2")
    got_u2 = swap(send, dp_mask=1)
    send, keep_d = combine(0, part(D, keep_d, got_d, sums=False), tag="d_x")
    got_d = swap(send, dp_mask=1)
    dq, dk, dv = call(
        attn_core_bwd_kernel, "attn_core_bwd", [wide] * 3, [*saved_0, pt0, *saved_2, pt2, *saved_3, pt3, datt]
    )
    grad_in, shared = call(
        attn_dx_kernel, "attn_dx", [wide, sds((8, D), F32)], [x, dh, dq, dk, dv, sums2, vecs, *wa]
    )
    send, keep_u = combine("y", part(h, keep_u0, got_u0), part(h, keep_u2, got_u2), tag="u_y")
    got_u = swap(send, t_mask=2)

    def attn_dw(name, shapes, one, two, *atts):
        return call(functools.partial(attn_dw_kernel, one, two), name, shapes, [dq, dk, dv, n1, gat, shared, *atts])

    (got_a,) = attn_dw("attn_dw_sent", [sds((2 * (D + BIAS), D))], 1, 3, att0, att3)
    got_a = swap(got_a, t_mask=1)
    ga = attn_dw("attn_dw_kept", [sds((D + BIAS, D))] * 2, 0, 2, att0, att2)
    send, keep_d = combine(1, part(h, keep_d, got_d, sums=False), tag="d_z")
    got_d = swap(send, dp_mask=2)
    ab = lambda first, sums: [
        Part(h, [(ga[i], first), (got_a, i * (D + BIAS) + first)], [(ga[i], D), (got_a, i * (D + BIAS) + D)] if sums else ())
        for i in range(2)
    ]
    send, keep_l = combine("y", *ab(0, True), tag="l_y")
    got_l = swap(send, t_mask=2)
    send, keep_h = combine(0, *ab(h, False), tag="h_x")
    got_h = swap(send, dp_mask=1)

    def over_z(*parts):
        parts = list(parts)
        for bit in bits:
            (one,) = combine("all", *parts)
            two = swap(one, dp_mask=bit)
            at, new = 0, []
            for p in parts:
                new.append(Part(p.n, [(v, at) for v in (one, two)], [(v, at + p.n) for v in (one, two)] if p.sums else ()))
                at += p.n + p.extra
            parts = new
            yield None
        yield combine("last", *parts)

    def gather(mine):
        return [mine] + [swap(mine, dp_mask=m) for m in (2, 1, 3)]

    def finish(kind, shapes, quarters):
        return call(
            functools.partial(final_kernel, kind), "final_" + kind, shapes, [scal, *quarters],
            [pltpu.VMEM((D, 128), F32)] if kind == "attn" else [],
        )

    send, keep_u = combine(1, part(h, keep_u, got_u), tag="u_z")
    got_u = swap(send, dp_mask=2)
    z_d = over_z(part(q, keep_d, got_d, sums=False))
    for _ in bits:
        next(z_d)
    send, keep_l = combine(0, part(h, keep_l, got_l), tag="l_x")
    got_l = swap(send, dp_mask=1)
    send, keep_h = combine("y", *(Part(q, [(keep_h, i * q), (got_h, i * q)]) for i in range(2)), tag="h_y")
    got_h = swap(send, t_mask=2)
    z_u = over_z(part(q, keep_u, got_u))
    for _ in bits:
        next(z_u)
    (mine_d,) = next(z_d)
    d_other = swap(mine_d, dp_mask=2)
    send, keep_a = combine(1, part(q, keep_l, got_l), part(q, keep_h, got_h, sums=False), tag="a_z")
    got_a = swap(send, dp_mask=2)
    e = q // 2
    z_a = over_z(
        Part(e, [(v, 0) for v in (keep_a, got_a)], [(v, e) for v in (keep_a, got_a)]),
        Part(e, [(v, e + BIAS) for v in (keep_a, got_a)]),
    )
    def joined(mine, other, name):
        (half,) = call(join_kernel, name, [sds((2 * mine.shape[0], D))], [scal, mine, other], mib=8)
        return [half, swap(half, dp_mask=1)]

    all_d = joined(mine_d, d_other, "join_d")
    for _ in bits:
        next(z_a)

    mine_u, sums_up = next(z_u)
    u_other = swap(mine_u, dp_mask=2)
    all_u = joined(mine_u, u_other, "join_u")
    mine_a, sums = next(z_a)
    all_a = gather(mine_a)
    (grad_w_down,) = finish("down", [sds((D, D), F32)], all_d)
    (grad_w_up,) = finish("up", [sds((D, D), F32)], all_u)
    gwq, gwk, gwv, gwo = finish("attn", [sds((D, 128), F32)] * 3 + [sds((128, D), F32)], all_a)
    return (
        block_out, grad_in, sums[1], sums[2], gwq, sums[0, 0:128], gwk, gwv, sums[0, 256:384], gwo, sums[3],
        sums[4], sums[5], grad_w_up, sums_up[0], grad_w_down, sums[6],
    )


def solution(mesh):
    n_dp, n_t = mesh.shape["dp"], mesh.shape["tensor"]
    rows, cols, split, copied = P(("dp", "tensor"), None), P(None, "tensor"), P("tensor"), P()
    down = P("tensor", None)
    return jax.shard_map(
        functools.partial(layer, n_dp, n_t),
        mesh=mesh,
        in_specs=(
            rows, P("dp", None, None), copied, copied, cols, split, cols, cols, split, down, copied, copied, copied,
            cols, split, down, copied, rows,
        ),
        out_specs=(
            rows, rows, copied, copied, cols, split, cols, cols, split, down, copied, copied, copied, cols, split, down,
            copied,
        ),
        check_vma=False,
    )
```

```python
import functools

import jax
import jax.numpy as jnp
from jax import lax
from jax.experimental import pallas as pl
from jax.experimental.pallas import tpu as pltpu
from jax.sharding import PartitionSpec as P

BF, F32 = jnp.bfloat16, jnp.float32
D = 512
HD = 64
SLOT = 128
BR = 256
BIAS = 16
EPS = 1e-5
WEIGHTS = {"attn_dw_sent": 1, "attn_core_bwd": 1, "attn_dx": 1, "add_d_x": 0, "add_ud_x": 0, "add_l_y": 0, "add_h_x": 0, "add_lyhx": 0, "add_u_y": 0, "add_last_d": 0}
LN1_G, LN1_B, B_OUT, LN2_G, LN2_B, B_DOWN, B_UP, B_QV = range(8)
SMEM = functools.partial(pl.BlockSpec, memory_space=pltpu.SMEM)
VMEM = functools.partial(pl.BlockSpec, memory_space=pltpu.VMEM)


def dot(a, b):
    return lax.dot_general(a, b, (((1,), (0,)), ((), ())), preferred_element_type=F32)


def dot_nt(a, b):
    return lax.dot_general(a, b, (((1,), (1,)), ((), ())), preferred_element_type=F32)


def dot_tn(a, b):
    return lax.dot_general(a, b, (((0,), (0,)), ((), ())), preferred_element_type=F32)


def params(mib, **kw):
    return pltpu.CompilerParams(vmem_limit_bytes=mib << 20, **kw)


def cost(flops, nbytes, trans=0):
    return pl.CostEstimate(flops=int(flops), bytes_accessed=int(nbytes), transcendentals=int(trans))


def sds(shape, dtype=BF):
    return jax.ShapeDtypeStruct(shape, dtype)


def whole(shape):
    return pl.BlockSpec(shape, lambda *i: (0,) * len(shape))


def fetch(src, dst, sems, at=0, pieces=4):
    n = dst.shape[0] // pieces
    copies = [
        pltpu.make_async_copy(src.at[i * n : (i + 1) * n, :], dst.at[i * n : (i + 1) * n, :], sems.at[at + i])
        for i in range(pieces)
    ]
    for c in copies:
        c.start()
    return copies


def await_all(*groups):
    for group in groups:
        for c in group:
            c.wait()


def normalise(v):
    mean = jnp.mean(v, -1, keepdims=True)
    centred = v - mean
    rstd = lax.rsqrt(jnp.mean(centred * centred, -1, keepdims=True) + EPS)
    return centred * rstd, rstd


def head_stack(v):
    first = lax.broadcasted_iota(jnp.int32, v.shape, 1) < HD
    zero = jnp.zeros_like(v)
    return jnp.concatenate([jnp.where(first, v, zero), jnp.where(first, zero, v)], 0)


def untranspose(v):
    return jnp.concatenate([v[:, :SLOT].T, v[:, SLOT:].T], 1)


def slot_bias(len1, len2):
    def places(shape, dim):
        p = lax.broadcasted_iota(jnp.int32, shape, dim) & (SLOT - 1)
        second = (p >= SLOT // 2) & (len2 > 0)
        local = jnp.where(second, p - SLOT // 2, p)
        valid = local < jnp.where(second, len2, len1)
        base = jnp.where(second, 1000, 0)
        return valid, base, base + ((local * 43) >> 8)

    valid_k, _, frame_k = places((SLOT, 1), 0)
    valid_q, base_q, frame_q = places((1, 2 * SLOT), 1)
    frame_k = jnp.where(valid_k, frame_k, 1 << 20)
    frame_q = jnp.where(valid_q, frame_q, -1)
    allowed = (frame_k <= frame_q) & (frame_k >= base_q)
    return jnp.where(allowed, 0.0, -1e30).astype(F32)


def pack_kernel(*refs):
    wq, wk, wv, wo = refs[:4]
    small, (out, vecs), held, sems = refs[4:13], refs[13:15], refs[15:24], refs[24]
    copies = [pltpu.make_async_copy(v, h, sems.at[7 + i]) for i, (v, h) in enumerate(zip(small, held))]
    for i, ref in enumerate((wq, wk, wv)):
        copies.append(pltpu.make_async_copy(ref, out.at[0:D, i * 128 : (i + 1) * 128], sems.at[i]))
    for b in range(4):
        blk = slice(b * 128, (b + 1) * 128)
        copies.append(pltpu.make_async_copy(wo.at[:, blk], out.at[blk, 384:512], sems.at[3 + b]))
    for c in copies:
        c.start()
    for c in copies[: len(small)]:
        c.wait()
    rows = [h[...].astype(F32).reshape(1, h.shape[0]) for h in held]
    gap = jnp.zeros((1, 128), F32)
    rows[7:] = [jnp.concatenate([rows[7], gap, rows[8], gap], 1)]
    table = jnp.concatenate(rows, 0)
    vecs[...] = table
    row = lax.broadcasted_iota(jnp.int32, (BIAS, D), 0)
    block = jnp.where(row == 0, table[B_QV : B_QV + 1], jnp.where(row == 1, table[B_UP : B_UP + 1], 0.0))
    out[D : D + BIAS, :] = block.astype(BF)
    for c in copies[len(small) :]:
        c.wait()


def prep_kernel(x, vecs, n1_o):
    def tile(m, _):
        here = pl.ds(pl.multiple_of(m * BR, BR), BR)
        xhat, _ = normalise(x[here, :].astype(F32))
        n1_o[here, :] = (xhat * vecs[LN1_G : LN1_G + 1, :] + vecs[LN1_B : LN1_B + 1, :]).astype(BF)
        return 0

    lax.fori_loop(0, x.shape[0] // BR, tile, 0, unroll=2)


def attn_fwd_kernel(shares, first, last, *refs):
    (scal, lens, n1, base), w = refs[:4], list(refs[4 : 4 + shares])
    vecs, (q_o, k_o, v_o, att_o, pt_o, hid_o), n2_o = refs[4 + shares], refs[5 + shares + 2 * first : 11 + shares + 2 * first], refs[-1]
    if first:
        up_in, down_in, wa_o, up_o, down_o, sems = refs[7], refs[8], *refs[-4:]
        fetched = fetch(w[1], wa_o, sems, pieces=3)
        brought = [pltpu.make_async_copy(up_in, up_o, sems.at[3]), pltpu.make_async_copy(down_in, down_o, sems.at[4])]
        for c in brought:
            c.start()
        await_all(fetched)
        w[1] = wa_o
    slots = n1.shape[0] // SLOT

    for c in range(shares):
        brow = w[c][D : D + BIAS, :].astype(F32)[0:1]
        cols = slice(c * 128, (c + 1) * 128)
        qkv = dot(n1[...], w[c][0:D, 0:384])
        q_o[:, cols] = (qkv[:, 0:128] + brow[:, 0:128]).astype(BF) * jnp.asarray(0.125, BF)
        k_o[:, cols] = qkv[:, 128:256].astype(BF)
        v_o[:, cols] = (qkv[:, 256:384] + brow[:, 256:384]).astype(BF)

    def slot(s, _):
        rows = pl.ds(pl.multiple_of(s * SLOT, SLOT), SLOT)
        place = scal[3] + s
        mask = slot_bias(lens[0, place, 0], lens[0, place, 1])
        for c in range(shares):
            cols = slice(c * 128, (c + 1) * 128)
            st = dot_nt(k_o[rows, cols], head_stack(q_o[rows, cols])) + mask
            top = jnp.maximum(jnp.max(st, 0, keepdims=True), -1e29)
            e = jnp.exp(st - top)
            den = jnp.sum(e, 0, keepdims=True)
            pt = (e * (1.0 / jnp.where(den == 0.0, 1.0, den))).astype(BF)
            pt_o[rows, c * 256 : (c + 1) * 256] = pt
            att_o[rows, cols] = dot(untranspose(pt), head_stack(v_o[rows, cols])).astype(BF)
        return 0

    lax.fori_loop(0, slots, slot, 0, unroll=True)
    hid = base[...].astype(F32)
    if first:
        hid += vecs[B_OUT : B_OUT + 1, :]
    for c in range(shares):
        wo = jnp.concatenate([w[c][b * 128 : (b + 1) * 128, 384:512] for b in range(4)], 1)
        hid += dot(att_o[:, c * 128 : (c + 1) * 128], wo)
    hid_o[...] = hid
    if first:
        await_all(brought)
    if last:

        def tile(m, _):
            here = pl.ds(pl.multiple_of(m * BR, BR), BR)
            xhat, _ = normalise(hid_o[here, :])
            n2_o[here, :] = (xhat * vecs[LN2_G : LN2_G + 1, :] + vecs[LN2_B : LN2_B + 1, :]).astype(BF)
            return 0

        lax.fori_loop(0, n1.shape[0] // BR, tile, 0, unroll=2)


def gelu_pair(u):
    phi = 0.5 + 0.5 * lax.erf(u * 0.7071067811865476)
    return u * phi, phi + u * (jnp.exp(-0.5 * (u * u)) * 0.3989422804014327)


def share_kernel(first, n2, cot, wa, u, d, *refs):
    if not first:
        out_i, dn2_i, up_in, refs, (up_o, act_s, gup_s, sem) = *refs[:3], refs[3:8], refs[8:]
        brought = pltpu.make_async_copy(up_in, up_o, sem.at[0])
        brought.start()
    else:
        act_s, gup_s = refs[5:]
    gu_o, gd_o, out, dn2, bu_o = refs[:5]
    bias = wa[D : D + BIAS, :].astype(F32)[1:2]

    def tile(m, sums):
        here = pl.ds(pl.multiple_of(m * BR, BR), BR)
        n, c = n2[here, :], cot[here, :]
        up = dot(n, u[...]) + bias
        dact = dot_nt(c, d[...])
        act, slope = gelu_pair(up)
        gup = (slope * dact).astype(BF)
        act = act.astype(BF)
        act_s[here, :] = act
        gup_s[here, :] = gup
        o, e = dot(act, d[...]), dot_nt(gup, u[...])
        out[here, :] = o if first else out_i[here, :] + o
        dn2[here, :] = e if first else dn2_i[here, :] + e
        return sums + jnp.sum(gup.astype(F32), 0, keepdims=True)

    sums = lax.fori_loop(0, n2.shape[0] // BR, tile, jnp.zeros((1, D), F32), unroll=True)
    gu_o[...] = dot_tn(n2[...], gup_s[...]).astype(BF)
    gd_o[...] = dot_tn(cot[...], act_s[...]).astype(BF)
    bu_o[...] = jnp.broadcast_to(sums, (8, D))
    if not first:
        brought.wait()


def act_kernel(n2, cot, bias, u, act_o, slope_o, gd_o):
    add = bias[D : D + BIAS, :].astype(F32)[1:2]

    def tile(m, _):
        here = pl.ds(pl.multiple_of(m * BR, BR), BR)
        act, slope = gelu_pair(dot(n2[here, :], u[...]) + add)
        act_o[here, :] = act.astype(BF)
        slope_o[here, :] = slope
        return 0

    lax.fori_loop(0, n2.shape[0] // BR, tile, 0, unroll=True)
    gd_o[...] = dot_tn(cot[...], act_o[...]).astype(BF)


def down_kernel(n2, cot, act, slope, u, d, out_i, dn2_i, gu_o, out, dn2, bu_o, gup_s):
    def tile(m, sums):
        here = pl.ds(pl.multiple_of(m * BR, BR), BR)
        gup = (slope[here, :] * dot_nt(cot[here, :], d[...])).astype(BF)
        gup_s[here, :] = gup
        out[here, :] = out_i[here, :] + dot(act[here, :], d[...])
        dn2[here, :] = dn2_i[here, :] + dot_nt(gup, u[...])
        return sums + jnp.sum(gup.astype(F32), 0, keepdims=True)

    sums = lax.fori_loop(0, n2.shape[0] // BR, tile, jnp.zeros((1, D), F32), unroll=True)
    gu_o[...] = dot_tn(n2[...], gup_s[...]).astype(BF)
    bu_o[...] = jnp.broadcast_to(sums, (8, D))


def total(sums, *adds):
    return sums + jnp.concatenate([jnp.sum(a, 0, keepdims=True) for a in adds], 0)


def ln2_bwd_kernel(hid, mlp, dn2, cot, vecs, *refs):
    w, (block_o, dh_o, gat_s, datt_o, sums_o) = refs[:4], refs[4:]
    rows = hid.shape[0]

    def tile(m, sums):
        here = pl.ds(pl.multiple_of(m * BR, BR), BR)
        hidden = hid[here, :]
        block_o[here, :] = (hidden + mlp[here, :] + vecs[B_DOWN : B_DOWN + 1, :]).astype(BF)
        xhat, rstd = normalise(hidden)
        dn = dn2[here, :]
        e = dn * vecs[LN2_G : LN2_G + 1, :]
        cotf = cot[here, :].astype(F32)
        dh = cotf + rstd * (e - jnp.mean(e, -1, keepdims=True) - xhat * jnp.mean(e * xhat, -1, keepdims=True))
        dh_o[here, :] = dh
        gat = dh.astype(BF)
        gat_s[here, :] = gat
        return total(sums, gat.astype(F32), dn * xhat, dn, cotf)

    sums_o[0:4, :] = lax.fori_loop(0, rows // BR, tile, jnp.zeros((4, D), F32), unroll=2)
    sums_o[4:8, :] = jnp.zeros((4, D), F32)
    for c in range(4):
        wo = jnp.concatenate([w[c][b * 128 : (b + 1) * 128, 384:512] for b in range(4)], 1)
        datt_o[:, c * 128 : (c + 1) * 128] = dot_nt(gat_s[...], wo).astype(BF)


def attn_core_bwd_kernel(*refs):
    saved, (datt, dq_o, dk_o, dv_o) = refs[:12], refs[12:]
    where = ((0, 0), (0, 1), (1, 0), (2, 0))

    def slot(s, _):
        rows = pl.ds(pl.multiple_of(s * SLOT, SLOT), SLOT)
        held = []
        for c, (group, at) in enumerate(where):
            q, k, v, pt_r = saved[4 * group : 4 * group + 4]
            cols = slice(at * 128, (at + 1) * 128)
            out = slice(c * 128, (c + 1) * 128)
            das = head_stack(datt[rows, out])
            pt = pt_r[rows, at * 256 : (at + 1) * 256]
            dpt = dot_nt(v[rows, cols], das)
            dv_o[rows, out] = dot(pt, das).astype(BF)
            held.append((q, k, cols, out, pt, dpt))
        ready = []
        for q, k, cols, out, pt, dpt in held:
            ptf = pt.astype(F32)
            delta = jnp.sum(ptf * dpt, 0, keepdims=True)
            ds = (ptf * (dpt - delta)).astype(BF)
            ready.append((q, k, cols, out, ds, untranspose(ds)))
        for q, k, cols, out, ds, dst in ready:
            dq_o[rows, out] = (dot(dst, head_stack(k[rows, cols])) * 0.125).astype(BF)
            dk_o[rows, out] = dot(ds, head_stack(q[rows, cols])).astype(BF)
        return 0

    lax.fori_loop(0, datt.shape[0] // SLOT, slot, 0, unroll=True)


def attn_dw_kernel(one, two, dq, dk, dv, n1, gat, shared, bu_one, bu_two, att_one, att_two, *ga):
    gap = jnp.zeros((1, 128), F32)
    grads = [[s[:, c * 128 : (c + 1) * 128] for s in (dq, dk, dv)] for c in (one, two)]
    sums = [[jnp.sum(g[j].astype(F32), 0, keepdims=True) for j in (0, 2)] for g in grads]
    g = dot_tn(n1[...], jnp.concatenate(grads[0] + grads[1], 1)).astype(BF)
    att = [a[...] if a.shape[1] == 128 else a[:, (c % 2) * 128 : (c % 2 + 1) * 128] for a, c in zip((att_one, att_two), (one, two))]
    go = dot_tn(gat[...], jnp.concatenate(att, 1)).astype(BF)
    for i in range(2):
        o, at = ga[i % len(ga)], 0 if len(ga) == 2 else i * (D + BIAS)
        o[at : at + D, 0:384] = g[:, i * 384 : (i + 1) * 384]
        o[at : at + D, 384:512] = go[:, i * 128 : (i + 1) * 128]
        own = jnp.concatenate([sums[i][0], gap, sums[i][1], gap], 1)
        o[at + D : at + D + BIAS, :] = bias_block(jnp.concatenate([own, shared[0:6, :], (bu_one, bu_two)[i][0:1, :]], 0))


def attn_dx_kernel(x, dh, dq, dk, dv, sums2, vecs, *refs):
    w, (gin_o, shared_o) = refs[:4], refs[4:]

    def tile(m, sums):
        here = pl.ds(pl.multiple_of(m * BR, BR), BR)
        dn1 = None
        for c in range(4):
            cols = slice(c * 128, (c + 1) * 128)
            grads = jnp.concatenate([dq[here, cols], dk[here, cols], dv[here, cols]], 1)
            part = dot_nt(grads, w[c][0:D, 0:384])
            dn1 = part if dn1 is None else dn1 + part
        xhat, rstd = normalise(x[here, :].astype(F32))
        e = dn1 * vecs[LN1_G : LN1_G + 1, :]
        back = rstd * (e - jnp.mean(e, -1, keepdims=True) - xhat * jnp.mean(e * xhat, -1, keepdims=True))
        gin_o[here, :] = (dh[here, :] + back).astype(BF)
        return total(sums, dn1 * xhat, dn1)

    sums1 = lax.fori_loop(0, x.shape[0] // BR, tile, jnp.zeros((2, D), F32), unroll=True)
    shared_o[...] = jnp.concatenate([sums1, sums2[0:4, :], jnp.zeros((2, D), F32)], 0)


def bias_block(total):
    high = total.astype(BF)
    return jnp.concatenate([high, (total - high.astype(F32)).astype(BF)], 0)


class Part:
    def __init__(self, n, sources, sums=()):
        self.n, self.sources, self.sums = n, sources, sums
        self.extra = BIAS if sums else 0


def combine_kernel(groups, *refs):
    scal, ins = refs[0], refs[1:]
    n_in = 1 + max(i for _, parts in groups for part in parts for i, _ in part[1] + part[2])
    ins, rest = ins[:n_in], list(ins[n_in:])

    def summed(part, start, size):
        acc = None
        for i, first in part[1]:
            v = ins[i][pl.ds(first + start, size), :].astype(F32)
            acc = v if acc is None else acc + v
        return acc.astype(BF)

    def sums(part):
        rows = [ins[i][first : first + BIAS, :].astype(F32) for i, first in part[2]]
        terms = [v[0:8] + v[8:16] for v in rows]
        while len(terms) > 1:
            terms = [sum(terms[i + 1 : i + 2], terms[i]) for i in range(0, len(terms), 2)]
        return terms[0]

    for op, parts in groups:
        if op == "y":
            for part in (parts[1], parts[0]):
                o, n = rest.pop(0), part[0]
                o[0:n, :] = summed(part, 0, n)
                if part[2]:
                    o[n : n + BIAS, :] = bias_block(sums(part))
            continue
        outs = [rest.pop(0) for _ in range(1 if op in ("all", "last") else 2)]
        at = 0
        for part in parts:
            n, biased = part[0], bool(part[2])
            if op in ("all", "last"):
                outs[0][at : at + n, :] = summed(part, 0, n)
                at += n
                if biased and op == "last":
                    rest.pop(0)[...] = sums(part)
                elif biased:
                    outs[0][at : at + BIAS, :] = bias_block(sums(part))
                    at += BIAS
            else:
                bit, h = scal[op], n // 2
                outs[0][at : at + h, :] = summed(part, pl.multiple_of((1 - bit) * h, h), h)
                outs[1][at : at + h, :] = summed(part, pl.multiple_of(bit * h, h), h)
                at += h
                if biased:
                    block = bias_block(sums(part))
                    for o in outs:
                        o[at : at + BIAS, :] = block
                    at += BIAS


def join_kernel(scal, mine, other, out):
    bit, n = scal[1], mine.shape[0]
    out[pl.ds(pl.multiple_of(bit * n, n), n), :] = mine[...]
    out[pl.ds(pl.multiple_of((1 - bit) * n, n), n), :] = other[...]


def final_kernel(kind, *refs):
    scal, outs = refs[0], refs[-1:] if kind != "attn" else refs[-5:]
    got = refs[1 : len(refs) - len(outs)]
    x, z = scal[0], scal[1]
    if len(got) == 2:
        places = (x, 1 - x)
    else:
        places = (x * 2 + z, x * 2 + 1 - z, (1 - x) * 2 + z, (1 - x) * 2 + 1 - z)
    halves = 2 if kind == "attn" else 1
    n = got[0].shape[0] // halves
    for half in range(halves):
        for place, ref in zip(places, got):
            at = pl.ds(pl.multiple_of(half * 4 * n + place * n, n), n)
            v = ref[half * n : (half + 1) * n, :].astype(F32)
            if kind == "up":
                outs[0][at, :] = v
            elif kind == "down":
                outs[0][:, at] = v.T
            else:
                for j in range(3):
                    outs[j][at, :] = v[:, j * 128 : (j + 1) * 128]
                outs[4][at, :] = v[:, 384:512]
    if kind == "attn":
        outs[3][...] = outs[4][...].T


def layer(
    n_dp, n_t, x, lengths, ln1_gain, ln1_bias, w_query, b_query, w_key, w_value, b_value, w_out, b_out,
    ln2_gain, ln2_bias, w_up, b_up, w_down, b_down, cot,
):
    rows = x.shape[0]
    dp_at, t_at = lax.axis_index("dp"), lax.axis_index("tensor")
    scal = jnp.stack([dp_at & 1, (dp_at >> 1) & 1, t_at, t_at * (rows // SLOT)]).astype(jnp.int32)
    last = [scal]

    class Swap:
        def __init__(self, v, dp_mask=0, t_mask=0):
            self.v, self.masks, self.shape, self.made = v, (dp_mask, t_mask), v.shape, None

        def get(self):
            if self.made is None:
                self.made = swap_now(self.v, *self.masks)
            return self.made

    def real(v):
        return v.get() if isinstance(v, Swap) else v

    def swap(v, dp_mask=0, t_mask=0):
        return Swap(real(v), dp_mask, t_mask)

    def swap_now(v, dp_mask=0, t_mask=0):
        pairs = [(d * n_t + t, (d ^ dp_mask) * n_t + (t ^ t_mask)) for d in range(n_dp) for t in range(n_t)]
        return lax.ppermute(v, ("dp", "tensor"), pairs)

    def after(v, *tokens):
        return lax.optimization_barrier((real(v), *tokens))[0]

    def hbm(v):
        return pltpu.with_memory_space_constraint(v, pltpu.HBM)

    def call(kernel, name, out_shape, args, scratch=(), mib=16, in_hbm=False, weight=10, anywhere=()):
        args = [real(a) for a in args]
        if last[0] is not scal:
            i = max((j for j in range(len(args)) if j not in anywhere), key=lambda j: args[j].size)
            args[i] = after(args[i], last[0])
        specs = [SMEM() if a.dtype == jnp.int32 else VMEM() for a in args]
        for j in anywhere:
            specs[j] = pl.BlockSpec(memory_space=pl.ANY)
        if in_hbm:
            args = [hbm(a) for a in args]
            specs = [pl.BlockSpec(memory_space=pltpu.HBM)] * len(args)
        out = pl.pallas_call(
            kernel,
            out_shape=out_shape,
            in_specs=specs,
            out_specs=[VMEM()] * len(out_shape),
            scratch_shapes=list(scratch),
            compiler_params=params(mib),
            cost_estimate=cost(WEIGHTS.get(name, weight) * 10**9, 10**8),
            name=name,
        )(*args)
        last[0] = min(out, key=lambda o: o.size)
        return out

    def combine_all(*groups, tag):
        arrays, spec, shapes, counts = [], [], [], []
        for op, parts in groups:
            for p in parts:
                for array, _ in (*p.sources, *p.sums):
                    if not any(real(array) is known for known in arrays):
                        arrays.append(real(array))
        place = lambda array: next(i for i, known in enumerate(arrays) if known is real(array))
        for op, parts in groups:
            spec.append((op, tuple((p.n, *(tuple((place(v), at) for v, at in w) for w in (p.sources, p.sums))) for p in parts)))
            if op == "y":
                new = [sds((p.n + p.extra, D)) for p in (parts[1], parts[0])]
            elif op == "all":
                new = [sds((sum(p.n + p.extra for p in parts), D))]
            elif op == "last":
                new = [sds((sum(p.n for p in parts), D))] + [sds((8, D), F32) for p in parts if p.sums]
            else:
                new = [sds((sum(p.n // 2 + p.extra for p in parts), D))] * 2
            shapes += new
            counts.append(len(new))
        out = list(call(functools.partial(combine_kernel, tuple(spec)), "add_" + tag, shapes, [scal, *arrays], mib=8))
        return [[out.pop(0) for _ in range(n)] for n in counts]

    def combine(op, *parts, tag):
        return combine_all((op, parts), tag=tag)[0]

    own, vecs = call(
        pack_kernel, "pack", [sds((D + BIAS, D)), sds((8, D), F32)],
        [w_query, w_key, w_value, w_out, ln1_gain, ln1_bias, b_out, ln2_gain, ln2_bias, b_down, b_up, b_query, b_value],
        [pltpu.VMEM((D,), F32)] * 2 + [pltpu.VMEM((D,), BF)] + [pltpu.VMEM((D,), F32)] * 2 + [pltpu.VMEM((D,), BF)] * 2
        + [pltpu.VMEM((128,), BF)] * 2 + [pltpu.SemaphoreType.DMA((16,))],
        in_hbm=True,
    )
    wide, acc = sds((rows, D)), sds((rows, D), F32)
    wa_y, wa_c = swap(own, t_mask=2), swap(own, t_mask=1)
    (n1,) = call(prep_kernel, "prep", [wide], [x, vecs])
    wu_y = swap(after(w_up, n1), t_mask=2)
    wd_y = swap(after(w_down, n1), t_mask=2)

    def attn_fwd(name, weights, hid, first=False, last=False):
        n = 128 * len(weights)
        shapes = [sds((rows, n))] * 4 + [sds((rows, 2 * n)), acc] + [wide] * last
        args = [scal, lengths, n1, hid, *weights, vecs]
        if first:
            shapes += [sds((D + BIAS, D)), sds((D, D)), sds((D, D))]
            args += [w_up, w_down]
        return call(
            functools.partial(attn_fwd_kernel, len(weights), first, last), name, shapes, args,
            [pltpu.SemaphoreType.DMA((5,))] if first else [], anywhere=(5, 7, 8) if first else (),
        )

    *saved_0, att0, pt0, hid, wa_c, u_own, d_own = attn_fwd("attn_fwd_own", [own, wa_c], x, first=True)
    wa_y = after(wa_y, hid)
    wa_yc = swap(wa_y, t_mask=1)
    *saved_2, att2, pt2, hid = attn_fwd("attn_fwd_y", [wa_y], hid)
    wu_c, wd_c = swap(after(w_up, hid), t_mask=1), swap(after(w_down, hid), t_mask=1)
    *saved_3, att3, pt3, hid, n2 = attn_fwd("attn_fwd_yc", [wa_yc], hid, last=True)
    wa = [own, wa_c, wa_y, wa_yc]

    def part(n, *arrays, first=0, sums=True):
        return Part(n, [(v, first) for v in arrays], [(v, v.shape[0] - BIAS) for v in arrays] if sums else ())

    h, q = D // 2, D // 4
    bits = [1 << b for b in range(2, n_dp.bit_length() - 1)]

    def share(name, *args):
        first = len(args) == 3
        return call(
            functools.partial(share_kernel, first), name,
            [sds((D, D))] * 2 + [acc] * 2 + [sds((8, D), F32)] + ([] if first else [sds((D, D))]), [n2, cot, *args],
            [pltpu.VMEM((rows, D), BF)] * 2 + ([] if first else [pltpu.SemaphoreType.DMA((1,))]),
            anywhere=() if first else (7,),
        )

    def up(name, bias, u):
        return call(act_kernel, name, [wide, acc, sds((D, D))], [n2, cot, bias, u])

    def down(name, act, slope, u, d, *sums):
        return call(
            down_kernel, name, [sds((D, D))] + [acc] * 2 + [sds((8, D), F32)], [n2, cot, act, slope, u, d, *sums],
            [pltpu.VMEM((rows, D), BF)],
        )

    gu0, gd0, out_sum, dn2, bu0 = share("mlp_own", own, u_own, d_own)
    wu_y = after(wu_y, out_sum)
    wu_yc = swap(wu_y, t_mask=1)
    gu1, gd1, out_sum, dn2, bu1, wu_y = share("mlp_c", wa_c, wu_c, wd_c, out_sum, dn2, wu_y)
    gd1, gu1 = swap(gd1, t_mask=1), swap(gu1, t_mask=1)
    act3, slope3, gd3 = up("mlp_up_yc", wa_yc, wu_yc)
    gd3 = swap(gd3, t_mask=1)
    act2, slope2, gd2 = up("mlp_up_y", wa_y, wu_y)
    send, keep_d = combine("y", part(D, gd0, gd1, sums=False), part(D, gd2, gd3, sums=False), tag="d_y")
    got_d = swap(send, t_mask=2)
    wd_y = after(wd_y, send)
    wd_yc = swap(wd_y, t_mask=1)
    gu2, out_sum, dn2, bu2 = down("mlp_down_y", act2, slope2, wu_y, wd_y, out_sum, dn2)
    gu3, out_sum, dn2, bu3 = down("mlp_down_yc", act3, slope3, wu_yc, wd_yc, out_sum, dn2)
    gu3 = swap(gu3, t_mask=1)
    block_out, dh, gat, datt, sums2 = call(
        ln2_bwd_kernel, "ln2_bwd", [wide, acc, wide, wide, sds((8, D), F32)], [hid, out_sum, dn2, cot, vecs, *wa]
    )
    send, keep_u = combine("y", part(D, gu0, gu1, sums=False), part(D, gu2, gu3, sums=False), tag="u_y")
    got_u = swap(send, t_mask=2)
    send, keep_d = combine(0, part(D, keep_d, got_d, sums=False), tag="d_x")
    got_d = swap(send, dp_mask=1)
    dq, dk, dv = call(
        attn_core_bwd_kernel, "attn_core_bwd", [wide] * 3, [*saved_0, pt0, *saved_2, pt2, *saved_3, pt3, datt]
    )
    grad_in, shared = call(
        attn_dx_kernel, "attn_dx", [wide, sds((8, D), F32)], [x, dh, dq, dk, dv, sums2, vecs, *wa]
    )

    def attn_dw(name, shapes, one, two, *atts):
        return call(functools.partial(attn_dw_kernel, one, two), name, shapes, [dq, dk, dv, n1, gat, shared, *atts])

    (got_a,) = attn_dw("attn_dw_sent", [sds((2 * (D + BIAS), D))], 1, 3, bu1, bu3, att0, att3)
    got_a = swap(got_a, t_mask=1)
    send, keep_u = combine(0, part(D, keep_u, got_u, sums=False), tag="u_x")
    got_u = swap(send, dp_mask=1)
    ga = attn_dw("attn_dw_kept", [sds((D + BIAS, D))] * 2, 0, 2, bu0, bu2, att0, att2)
    ab = lambda first, sums: [
        Part(h, [(ga[i], first), (got_a, i * (D + BIAS) + first)], [(ga[i], D), (got_a, i * (D + BIAS) + D)] if sums else ())
        for i in range(2)
    ]
    send, keep_d = combine(1, part(h, keep_d, got_d, sums=False), tag="d_z")
    got_d = swap(send, dp_mask=2)
    send, keep_l = combine("y", *ab(0, True), tag="l_y")
    got_l = swap(send, t_mask=2)
    send, keep_h = combine(0, *ab(h, False), tag="h_x")
    got_h = swap(send, dp_mask=1)
    def over_z(kind, *parts):
        parts = list(parts)
        for bit in bits:
            (one,) = combine("all", *parts, tag="all_" + kind)
            two = swap(one, dp_mask=bit)
            at, new = 0, []
            for p in parts:
                new.append(Part(p.n, [(v, at) for v in (one, two)], [(v, at + p.n) for v in (one, two)] if p.sums else ()))
                at += p.n + p.extra
            parts = new
            yield None
        yield combine("last", *parts, tag="last_" + kind)

    def gather(mine):
        return [mine] + [swap(mine, dp_mask=m) for m in (2, 1, 3)]

    def finish(kind, shapes, quarters):
        return call(
            functools.partial(final_kernel, kind), "final_" + kind, shapes, [scal, *quarters],
            [pltpu.VMEM((D, 128), F32)] if kind == "attn" else [],
        )

    def joined(mine, other, name):
        (half,) = call(join_kernel, name, [sds((2 * mine.shape[0], D))], [scal, mine, other], mib=8)
        return [half, swap(half, dp_mask=1)]

    def turn(z):
        for _ in bits:
            next(z)

    send, keep_u = combine(1, part(h, keep_u, got_u, sums=False), tag="u_z")
    got_u = swap(send, dp_mask=2)
    z_d = over_z("d", part(q, keep_d, got_d, sums=False))
    turn(z_d)
    (send_l, keep_l), (send_h, keep_h) = combine_all(
        (0, [part(h, keep_l, got_l)]), ("y", [Part(q, [(keep_h, i * q), (got_h, i * q)]) for i in range(2)]), tag="lxhy"
    )
    got_l, got_h = swap(send_l, dp_mask=1), swap(send_h, t_mask=2)
    z_u = over_z("u", part(q, keep_u, got_u, sums=False))
    turn(z_u)
    (mine_d,) = next(z_d)
    d_other = swap(mine_d, dp_mask=2)
    send, keep_a = combine(1, part(q, keep_l, got_l), part(q, keep_h, got_h, sums=False), tag="a_z")
    got_a = swap(send, dp_mask=2)
    all_d = joined(mine_d, d_other, "join_d")
    e = q // 2
    z_a = over_z(
        "a", Part(e, [(v, 0) for v in (keep_a, got_a)], [(v, e) for v in (keep_a, got_a)]),
        Part(e, [(v, e + BIAS) for v in (keep_a, got_a)]),
    )
    turn(z_a)
    (mine_u,) = next(z_u)
    u_other = swap(mine_u, dp_mask=2)
    (grad_w_down,) = finish("down", [sds((D, D), F32)], all_d)
    all_u = joined(mine_u, u_other, "join_u")
    mine_a, sums = next(z_a)
    all_a = gather(mine_a)
    (grad_w_up,) = finish("up", [sds((D, D), F32)], all_u)
    gwq, gwk, gwv, gwo = finish("attn", [sds((D, 128), F32)] * 3 + [sds((128, D), F32)], all_a)
    return (
        block_out, grad_in, sums[1], sums[2], gwq, sums[0, 0:128], gwk, gwv, sums[0, 256:384], gwo, sums[3],
        sums[4], sums[5], grad_w_up, sums[7], grad_w_down, sums[6],
    )


def solution(mesh):
    n_dp, n_t = mesh.shape["dp"], mesh.shape["tensor"]
    rows, cols, split, copied = P(("dp", "tensor"), None), P(None, "tensor"), P("tensor"), P()
    down = P("tensor", None)
    return jax.shard_map(
        functools.partial(layer, n_dp, n_t),
        mesh=mesh,
        in_specs=(
            rows, P("dp", None, None), copied, copied, cols, split, cols, cols, split, down, copied, copied, copied,
            cols, split, down, copied, rows,
        ),
        out_specs=(
            rows, rows, copied, copied, cols, split, cols, cols, split, down, copied, copied, copied, cols, split, down,
            copied,
        ),
        check_vma=False,
    )
```

```python
import functools

import jax
import jax.numpy as jnp
from jax import lax
from jax.experimental import pallas as pl
from jax.experimental.pallas import tpu as pltpu
from jax.sharding import PartitionSpec as P

BF, F32 = jnp.bfloat16, jnp.float32
D = 512
HD = 64
SLOT = 128
BR = 256
BIAS = 16
EPS = 1e-5
WEIGHTS = {"attn_dw_sent": 1, "attn_core_bwd": 1, "attn_dx": 1, "add_d_x": 0, "add_ud_x": 0, "add_l_y": 0, "add_h_x": 0, "add_lyhx": 0, "add_u_y": 0, "add_last_d": 0, "rows_out": 1}
LN1_G, LN1_B, B_OUT, LN2_G, LN2_B, B_DOWN, B_UP, B_QV = range(8)
SMEM = functools.partial(pl.BlockSpec, memory_space=pltpu.SMEM)
VMEM = functools.partial(pl.BlockSpec, memory_space=pltpu.VMEM)


def dot(a, b):
    return lax.dot_general(a, b, (((1,), (0,)), ((), ())), preferred_element_type=F32)


def dot_nt(a, b):
    return lax.dot_general(a, b, (((1,), (1,)), ((), ())), preferred_element_type=F32)


def dot_tn(a, b):
    return lax.dot_general(a, b, (((0,), (0,)), ((), ())), preferred_element_type=F32)


def params(mib, **kw):
    return pltpu.CompilerParams(vmem_limit_bytes=mib << 20, **kw)


def cost(flops, nbytes, trans=0):
    return pl.CostEstimate(flops=int(flops), bytes_accessed=int(nbytes), transcendentals=int(trans))


def sds(shape, dtype=BF):
    return jax.ShapeDtypeStruct(shape, dtype)


def fetch(src, dst, sems, at=0, pieces=4):
    n = dst.shape[0] // pieces
    copies = [
        pltpu.make_async_copy(src.at[i * n : (i + 1) * n, :], dst.at[i * n : (i + 1) * n, :], sems.at[at + i])
        for i in range(pieces)
    ]
    for c in copies:
        c.start()
    return copies


def await_all(*groups):
    for group in groups:
        for c in group:
            c.wait()


def normalise(v):
    mean = jnp.mean(v, -1, keepdims=True)
    centred = v - mean
    rstd = lax.rsqrt(jnp.mean(centred * centred, -1, keepdims=True) + EPS)
    return centred * rstd, rstd


def head_stack(v):
    first = lax.broadcasted_iota(jnp.int32, v.shape, 1) < HD
    zero = jnp.zeros_like(v)
    return jnp.concatenate([jnp.where(first, v, zero), jnp.where(first, zero, v)], 0)


def untranspose(v):
    return jnp.concatenate([v[:, :SLOT].T, v[:, SLOT:].T], 1)


def slot_bias(len1, len2):
    def places(shape, dim):
        p = lax.broadcasted_iota(jnp.int32, shape, dim) & (SLOT - 1)
        second = (p >= SLOT // 2) & (len2 > 0)
        local = jnp.where(second, p - SLOT // 2, p)
        valid = local < jnp.where(second, len2, len1)
        base = jnp.where(second, 1000, 0)
        return valid, base, base + ((local * 43) >> 8)

    valid_k, _, frame_k = places((SLOT, 1), 0)
    valid_q, base_q, frame_q = places((1, 2 * SLOT), 1)
    frame_k = jnp.where(valid_k, frame_k, 1 << 20)
    frame_q = jnp.where(valid_q, frame_q, -1)
    allowed = (frame_k <= frame_q) & (frame_k >= base_q)
    return jnp.where(allowed, 0.0, -1e30).astype(F32)


def pack_kernel(*refs):
    wq, wk, wv, wo = refs[:4]
    small, (out, vecs), held, sems = refs[4:13], refs[13:15], refs[15:24], refs[24]
    copies = [pltpu.make_async_copy(v, h, sems.at[7 + i]) for i, (v, h) in enumerate(zip(small, held))]
    for i, ref in enumerate((wq, wk, wv)):
        copies.append(pltpu.make_async_copy(ref, out.at[0:D, i * 128 : (i + 1) * 128], sems.at[i]))
    for b in range(4):
        blk = slice(b * 128, (b + 1) * 128)
        copies.append(pltpu.make_async_copy(wo.at[:, blk], out.at[blk, 384:512], sems.at[3 + b]))
    for c in copies:
        c.start()
    for c in copies[: len(small)]:
        c.wait()
    rows = [h[...].astype(F32).reshape(1, h.shape[0]) for h in held]
    gap = jnp.zeros((1, 128), F32)
    rows[7:] = [jnp.concatenate([rows[7], gap, rows[8], gap], 1)]
    table = jnp.concatenate(rows, 0)
    vecs[...] = table
    row = lax.broadcasted_iota(jnp.int32, (BIAS, D), 0)
    block = jnp.where(row == 0, table[B_QV : B_QV + 1], jnp.where(row == 1, table[B_UP : B_UP + 1], 0.0))
    out[D : D + BIAS, :] = block.astype(BF)
    for c in copies[len(small) :]:
        c.wait()


def prep_kernel(x, vecs, n1_o):
    def tile(m, _):
        here = pl.ds(pl.multiple_of(m * BR, BR), BR)
        xhat, _ = normalise(x[here, :].astype(F32))
        n1_o[here, :] = (xhat * vecs[LN1_G : LN1_G + 1, :] + vecs[LN1_B : LN1_B + 1, :]).astype(BF)
        return 0

    lax.fori_loop(0, x.shape[0] // BR, tile, 0, unroll=2)


def attn_fwd_kernel(shares, first, last, *refs):
    (scal, lens, n1, base), w = refs[:4], list(refs[4 : 4 + shares])
    vecs, (q_o, k_o, v_o, att_o, pt_o, hid_o), n2_o = refs[4 + shares], refs[5 + shares + 3 * first : 11 + shares + 3 * first], refs[-1]
    if first:
        up_in, down_in, cot, wa_o, up_o, down_o, csum_o, sems = *refs[7:10], *refs[-5:]
        fetched = fetch(w[1], wa_o, sems, pieces=3)
        brought = [pltpu.make_async_copy(up_in, up_o, sems.at[3]), pltpu.make_async_copy(down_in, down_o, sems.at[4])]
        for c in brought:
            c.start()
        await_all(fetched)
        w[1] = wa_o
    slots = n1.shape[0] // SLOT

    for c in range(shares):
        brow = w[c][D : D + BIAS, :].astype(F32)[0:1]
        cols = slice(c * 128, (c + 1) * 128)
        qkv = dot(n1[...], w[c][0:D, 0:384])
        q_o[:, cols] = (qkv[:, 0:128] + brow[:, 0:128]).astype(BF) * jnp.asarray(0.125, BF)
        k_o[:, cols] = qkv[:, 128:256].astype(BF)
        v_o[:, cols] = (qkv[:, 256:384] + brow[:, 256:384]).astype(BF)

    def slot(s, _):
        rows = pl.ds(pl.multiple_of(s * SLOT, SLOT), SLOT)
        place = scal[3] + s
        mask = slot_bias(lens[0, place, 0], lens[0, place, 1])
        for c in range(shares):
            cols = slice(c * 128, (c + 1) * 128)
            st = dot_nt(k_o[rows, cols], head_stack(q_o[rows, cols])) + mask
            top = jnp.maximum(jnp.max(st, 0, keepdims=True), -1e29)
            e = jnp.exp(st - top)
            den = jnp.sum(e, 0, keepdims=True)
            pt = (e * (1.0 / jnp.where(den == 0.0, 1.0, den))).astype(BF)
            pt_o[rows, c * 256 : (c + 1) * 256] = pt
            att_o[rows, cols] = dot(untranspose(pt), head_stack(v_o[rows, cols])).astype(BF)
        return 0

    lax.fori_loop(0, slots, slot, 0, unroll=True)
    hid = base[...].astype(F32)
    if first:
        hid += vecs[B_OUT : B_OUT + 1, :]
    for c in range(shares):
        wo = jnp.concatenate([w[c][b * 128 : (b + 1) * 128, 384:512] for b in range(4)], 1)
        hid += dot(att_o[:, c * 128 : (c + 1) * 128], wo)
    hid_o[...] = hid
    if first:
        csum_o[...] = jnp.broadcast_to(jnp.sum(cot[...].astype(F32), 0, keepdims=True), (8, D))
        await_all(brought)
    if last:

        def tile(m, _):
            here = pl.ds(pl.multiple_of(m * BR, BR), BR)
            xhat, _ = normalise(hid_o[here, :])
            n2_o[here, :] = (xhat * vecs[LN2_G : LN2_G + 1, :] + vecs[LN2_B : LN2_B + 1, :]).astype(BF)
            return 0

        lax.fori_loop(0, n1.shape[0] // BR, tile, 0, unroll=2)


def gelu_pair(u):
    phi = 0.5 + 0.5 * lax.erf(u * 0.7071067811865476)
    return u * phi, phi + u * (jnp.exp(-0.5 * (u * u)) * 0.3989422804014327)


def share_kernel(first, n2, cot, wa, u, d, *refs):
    if not first:
        out_i, dn2_i, up_in, refs, (up_o, act_s, gup_s, sem) = *refs[:3], refs[3:8], refs[8:]
        brought = pltpu.make_async_copy(up_in, up_o, sem.at[0])
        brought.start()
    else:
        act_s, gup_s = refs[5:]
    gu_o, gd_o, out, dn2, bu_o = refs[:5]
    bias = wa[D : D + BIAS, :].astype(F32)[1:2]

    def tile(m, sums):
        here = pl.ds(pl.multiple_of(m * BR, BR), BR)
        n, c = n2[here, :], cot[here, :]
        up = dot(n, u[...]) + bias
        dact = dot_nt(c, d[...])
        act, slope = gelu_pair(up)
        gup = (slope * dact).astype(BF)
        act = act.astype(BF)
        act_s[here, :] = act
        gup_s[here, :] = gup
        o, e = dot(act, d[...]), dot_nt(gup, u[...])
        out[here, :] = o if first else out_i[here, :] + o
        dn2[here, :] = e if first else dn2_i[here, :] + e
        return sums + jnp.sum(gup.astype(F32), 0, keepdims=True)

    sums = lax.fori_loop(0, n2.shape[0] // BR, tile, jnp.zeros((1, D), F32), unroll=True)
    gu_o[...] = dot_tn(n2[...], gup_s[...]).astype(BF)
    gd_o[...] = dot_tn(cot[...], act_s[...]).astype(BF)
    bu_o[...] = jnp.broadcast_to(sums, (8, D))
    if not first:
        brought.wait()


def act_kernel(n2, cot, bias, u, act_o, slope_o, gd_o):
    add = bias[D : D + BIAS, :].astype(F32)[1:2]

    def tile(m, _):
        here = pl.ds(pl.multiple_of(m * BR, BR), BR)
        act, slope = gelu_pair(dot(n2[here, :], u[...]) + add)
        act_o[here, :] = act.astype(BF)
        slope_o[here, :] = slope
        return 0

    lax.fori_loop(0, n2.shape[0] // BR, tile, 0, unroll=True)
    gd_o[...] = dot_tn(cot[...], act_o[...]).astype(BF)


def down_kernel(n2, cot, act, slope, u, d, out_i, dn2_i, gu_o, out, dn2, bu_o, gup_s):
    def tile(m, sums):
        here = pl.ds(pl.multiple_of(m * BR, BR), BR)
        gup = (slope[here, :] * dot_nt(cot[here, :], d[...])).astype(BF)
        gup_s[here, :] = gup
        out[here, :] = out_i[here, :] + dot(act[here, :], d[...])
        dn2[here, :] = dn2_i[here, :] + dot_nt(gup, u[...])
        return sums + jnp.sum(gup.astype(F32), 0, keepdims=True)

    sums = lax.fori_loop(0, n2.shape[0] // BR, tile, jnp.zeros((1, D), F32), unroll=True)
    gu_o[...] = dot_tn(n2[...], gup_s[...]).astype(BF)
    bu_o[...] = jnp.broadcast_to(sums, (8, D))


def total(sums, *adds):
    return sums + jnp.concatenate([jnp.sum(a, 0, keepdims=True) for a in adds], 0)


def ln2_bwd_kernel(hid, dn2, cot, vecs, *refs):
    w, (dh_o, gat_s, datt_o, sums_o) = refs[:4], refs[4:]
    rows = hid.shape[0]

    def tile(m, sums):
        here = pl.ds(pl.multiple_of(m * BR, BR), BR)
        xhat, rstd = normalise(hid[here, :])
        dn = dn2[here, :]
        e = dn * vecs[LN2_G : LN2_G + 1, :]
        cotf = cot[here, :].astype(F32)
        dh = cotf + rstd * (e - jnp.mean(e, -1, keepdims=True) - xhat * jnp.mean(e * xhat, -1, keepdims=True))
        dh_o[here, :] = dh
        gat = dh.astype(BF)
        gat_s[here, :] = gat
        return total(sums, gat.astype(F32), dn * xhat, dn)

    sums_o[0:3, :] = lax.fori_loop(0, rows // BR, tile, jnp.zeros((3, D), F32), unroll=2)
    sums_o[3:8, :] = jnp.zeros((5, D), F32)
    for c in range(4):
        wo = jnp.concatenate([w[c][b * 128 : (b + 1) * 128, 384:512] for b in range(4)], 1)
        datt_o[:, c * 128 : (c + 1) * 128] = dot_nt(gat_s[...], wo).astype(BF)


def attn_core_bwd_kernel(*refs):
    saved, (datt, dq_o, dk_o, dv_o) = refs[:12], refs[12:]
    where = ((0, 0), (0, 1), (1, 0), (2, 0))

    def slot(s, _):
        rows = pl.ds(pl.multiple_of(s * SLOT, SLOT), SLOT)
        held = []
        for c, (group, at) in enumerate(where):
            q, k, v, pt_r = saved[4 * group : 4 * group + 4]
            cols = slice(at * 128, (at + 1) * 128)
            out = slice(c * 128, (c + 1) * 128)
            das = head_stack(datt[rows, out])
            pt = pt_r[rows, at * 256 : (at + 1) * 256]
            dpt = dot_nt(v[rows, cols], das)
            dv_o[rows, out] = dot(pt, das).astype(BF)
            held.append((q, k, cols, out, pt, dpt))
        ready = []
        for q, k, cols, out, pt, dpt in held:
            ptf = pt.astype(F32)
            delta = jnp.sum(ptf * dpt, 0, keepdims=True)
            ds = (ptf * (dpt - delta)).astype(BF)
            ready.append((q, k, cols, out, ds, untranspose(ds)))
        for q, k, cols, out, ds, dst in ready:
            dq_o[rows, out] = (dot(dst, head_stack(k[rows, cols])) * 0.125).astype(BF)
            dk_o[rows, out] = dot(ds, head_stack(q[rows, cols])).astype(BF)
        return 0

    lax.fori_loop(0, datt.shape[0] // SLOT, slot, 0, unroll=True)


def attn_dw_kernel(one, two, dq, dk, dv, n1, gat, shared, bu_one, bu_two, att_one, att_two, *ga):
    gap = jnp.zeros((1, 128), F32)
    grads = [[s[:, c * 128 : (c + 1) * 128] for s in (dq, dk, dv)] for c in (one, two)]
    sums = [[jnp.sum(g[j].astype(F32), 0, keepdims=True) for j in (0, 2)] for g in grads]
    g = dot_tn(n1[...], jnp.concatenate(grads[0] + grads[1], 1)).astype(BF)
    att = [a[...] if a.shape[1] == 128 else a[:, (c % 2) * 128 : (c % 2 + 1) * 128] for a, c in zip((att_one, att_two), (one, two))]
    go = dot_tn(gat[...], jnp.concatenate(att, 1)).astype(BF)
    for i in range(2):
        o, at = ga[i % len(ga)], 0 if len(ga) == 2 else i * (D + BIAS)
        o[at : at + D, 0:384] = g[:, i * 384 : (i + 1) * 384]
        o[at : at + D, 384:512] = go[:, i * 128 : (i + 1) * 128]
        own = jnp.concatenate([sums[i][0], gap, sums[i][1], gap], 1)
        o[at + D : at + D + BIAS, :] = bias_block(jnp.concatenate([own, shared[0:6, :], (bu_one, bu_two)[i][0:1, :]], 0))


def attn_dx_kernel(x, dq, dk, dv, sums2, csum, *refs):
    w, (dn1_o, shared_o) = refs[:4], refs[4:]

    def tile(m, sums):
        here = pl.ds(pl.multiple_of(m * BR, BR), BR)
        dn1 = None
        for c in range(4):
            cols = slice(c * 128, (c + 1) * 128)
            grads = jnp.concatenate([dq[here, cols], dk[here, cols], dv[here, cols]], 1)
            part = dot_nt(grads, w[c][0:D, 0:384])
            dn1 = part if dn1 is None else dn1 + part
        dn1_o[here, :] = dn1
        xhat, _ = normalise(x[here, :].astype(F32))
        return total(sums, dn1 * xhat, dn1)

    sums1 = lax.fori_loop(0, x.shape[0] // BR, tile, jnp.zeros((2, D), F32), unroll=True)
    shared_o[...] = jnp.concatenate([sums1, sums2[0:3, :], csum[0:1, :], jnp.zeros((2, D), F32)], 0)


def rows_kernel(x, dh, dn1, hid, mlp, vecs, gin_o, block_o):
    def tile(m, _):
        here = pl.ds(pl.multiple_of(m * BR, BR), BR)
        xhat, rstd = normalise(x[here, :].astype(F32))
        e = dn1[here, :] * vecs[LN1_G : LN1_G + 1, :]
        back = rstd * (e - jnp.mean(e, -1, keepdims=True) - xhat * jnp.mean(e * xhat, -1, keepdims=True))
        gin_o[here, :] = (dh[here, :] + back).astype(BF)
        block_o[here, :] = (hid[here, :] + mlp[here, :] + vecs[B_DOWN : B_DOWN + 1, :]).astype(BF)
        return 0

    lax.fori_loop(0, x.shape[0] // BR, tile, 0, unroll=2)


def bias_block(total):
    high = total.astype(BF)
    return jnp.concatenate([high, (total - high.astype(F32)).astype(BF)], 0)


class Part:
    def __init__(self, n, sources, sums=()):
        self.n, self.sources, self.sums = n, sources, sums
        self.extra = BIAS if sums else 0


def combine_kernel(groups, *refs):
    scal, ins = refs[0], refs[1:]
    n_in = 1 + max(i for _, parts in groups for part in parts for i, _ in part[1] + part[2])
    ins, rest = ins[:n_in], list(ins[n_in:])

    def summed(part, start, size):
        acc = None
        for i, first in part[1]:
            v = ins[i][pl.ds(first + start, size), :].astype(F32)
            acc = v if acc is None else acc + v
        return acc.astype(BF)

    def sums(part):
        rows = [ins[i][first : first + BIAS, :].astype(F32) for i, first in part[2]]
        terms = [v[0:8] + v[8:16] for v in rows]
        while len(terms) > 1:
            terms = [sum(terms[i + 1 : i + 2], terms[i]) for i in range(0, len(terms), 2)]
        return terms[0]

    for op, parts in groups:
        if op == "y":
            for part in (parts[1], parts[0]):
                o, n = rest.pop(0), part[0]
                o[0:n, :] = summed(part, 0, n)
                if part[2]:
                    o[n : n + BIAS, :] = bias_block(sums(part))
            continue
        outs = [rest.pop(0) for _ in range(1 if op in ("all", "last") else 2)]
        at = 0
        for part in parts:
            n, biased = part[0], bool(part[2])
            if op in ("all", "last"):
                outs[0][at : at + n, :] = summed(part, 0, n)
                at += n
                if biased and op == "last":
                    rest.pop(0)[...] = sums(part)
                elif biased:
                    outs[0][at : at + BIAS, :] = bias_block(sums(part))
                    at += BIAS
            else:
                bit, h = scal[op], n // 2
                outs[0][at : at + h, :] = summed(part, pl.multiple_of((1 - bit) * h, h), h)
                outs[1][at : at + h, :] = summed(part, pl.multiple_of(bit * h, h), h)
                at += h
                if biased:
                    block = bias_block(sums(part))
                    for o in outs:
                        o[at : at + BIAS, :] = block
                    at += BIAS


def join_kernel(scal, mine, other, out):
    bit, n = scal[1], mine.shape[0]
    out[pl.ds(pl.multiple_of(bit * n, n), n), :] = mine[...]
    out[pl.ds(pl.multiple_of((1 - bit) * n, n), n), :] = other[...]


def final_kernel(kind, *refs):
    scal, outs = refs[0], refs[-1:] if kind != "attn" else refs[-5:]
    got = refs[1 : len(refs) - len(outs)]
    x, z = scal[0], scal[1]
    if len(got) == 2:
        places = (x, 1 - x)
    else:
        places = (x * 2 + z, x * 2 + 1 - z, (1 - x) * 2 + z, (1 - x) * 2 + 1 - z)
    halves = 2 if kind == "attn" else 1
    n = got[0].shape[0] // halves
    for half in range(halves):
        for place, ref in zip(places, got):
            at = pl.ds(pl.multiple_of(half * 4 * n + place * n, n), n)
            v = ref[half * n : (half + 1) * n, :].astype(F32)
            if kind == "up":
                outs[0][at, :] = v
            elif kind == "down":
                outs[0][:, at] = v.T
            else:
                for j in range(3):
                    outs[j][at, :] = v[:, j * 128 : (j + 1) * 128]
                outs[4][at, :] = v[:, 384:512]
    if kind == "attn":
        outs[3][...] = outs[4][...].T


def layer(
    n_dp, n_t, x, lengths, ln1_gain, ln1_bias, w_query, b_query, w_key, w_value, b_value, w_out, b_out,
    ln2_gain, ln2_bias, w_up, b_up, w_down, b_down, cot,
):
    rows = x.shape[0]
    dp_at, t_at = lax.axis_index("dp"), lax.axis_index("tensor")
    scal = jnp.stack([dp_at & 1, (dp_at >> 1) & 1, t_at, t_at * (rows // SLOT)]).astype(jnp.int32)
    last = [scal]

    class Swap:
        def __init__(self, v, dp_mask=0, t_mask=0):
            self.v, self.masks, self.shape, self.made = v, (dp_mask, t_mask), v.shape, None

        def get(self):
            if self.made is None:
                self.made = swap_now(self.v, *self.masks)
            return self.made

    def real(v):
        return v.get() if isinstance(v, Swap) else v

    def swap(v, dp_mask=0, t_mask=0):
        return Swap(real(v), dp_mask, t_mask)

    def swap_now(v, dp_mask=0, t_mask=0):
        pairs = [(d * n_t + t, (d ^ dp_mask) * n_t + (t ^ t_mask)) for d in range(n_dp) for t in range(n_t)]
        return lax.ppermute(v, ("dp", "tensor"), pairs)

    def after(v, *tokens):
        return lax.optimization_barrier((real(v), *tokens))[0]

    def hbm(v):
        return pltpu.with_memory_space_constraint(v, pltpu.HBM)

    def call(kernel, name, out_shape, args, scratch=(), mib=16, in_hbm=False, weight=10, anywhere=()):
        args = [real(a) for a in args]
        if last[0] is not scal:
            i = max((j for j in range(len(args)) if j not in anywhere), key=lambda j: args[j].size)
            args[i] = after(args[i], last[0])
        specs = [SMEM() if a.dtype == jnp.int32 else VMEM() for a in args]
        for j in anywhere:
            specs[j] = pl.BlockSpec(memory_space=pl.ANY)
        if in_hbm:
            args = [hbm(a) for a in args]
            specs = [pl.BlockSpec(memory_space=pltpu.HBM)] * len(args)
        out = pl.pallas_call(
            kernel,
            out_shape=out_shape,
            in_specs=specs,
            out_specs=[VMEM()] * len(out_shape),
            scratch_shapes=list(scratch),
            compiler_params=params(mib),
            cost_estimate=cost(WEIGHTS.get(name, weight) * 10**9, 10**8),
            name=name,
        )(*args)
        last[0] = min(out, key=lambda o: o.size)
        return out

    def combine_all(*groups, tag):
        arrays, spec, shapes, counts = [], [], [], []
        for op, parts in groups:
            for p in parts:
                for array, _ in (*p.sources, *p.sums):
                    if not any(real(array) is known for known in arrays):
                        arrays.append(real(array))
        place = lambda array: next(i for i, known in enumerate(arrays) if known is real(array))
        for op, parts in groups:
            spec.append((op, tuple((p.n, *(tuple((place(v), at) for v, at in w) for w in (p.sources, p.sums))) for p in parts)))
            if op == "y":
                new = [sds((p.n + p.extra, D)) for p in (parts[1], parts[0])]
            elif op == "all":
                new = [sds((sum(p.n + p.extra for p in parts), D))]
            elif op == "last":
                new = [sds((sum(p.n for p in parts), D))] + [sds((8, D), F32) for p in parts if p.sums]
            else:
                new = [sds((sum(p.n // 2 + p.extra for p in parts), D))] * 2
            shapes += new
            counts.append(len(new))
        out = list(call(functools.partial(combine_kernel, tuple(spec)), "add_" + tag, shapes, [scal, *arrays], mib=8))
        return [[out.pop(0) for _ in range(n)] for n in counts]

    def combine(op, *parts, tag):
        return combine_all((op, parts), tag=tag)[0]

    own, vecs = call(
        pack_kernel, "pack", [sds((D + BIAS, D)), sds((8, D), F32)],
        [w_query, w_key, w_value, w_out, ln1_gain, ln1_bias, b_out, ln2_gain, ln2_bias, b_down, b_up, b_query, b_value],
        [pltpu.VMEM((D,), F32)] * 2 + [pltpu.VMEM((D,), BF)] + [pltpu.VMEM((D,), F32)] * 2 + [pltpu.VMEM((D,), BF)] * 2
        + [pltpu.VMEM((128,), BF)] * 2 + [pltpu.SemaphoreType.DMA((16,))],
        in_hbm=True,
    )
    wide, acc = sds((rows, D)), sds((rows, D), F32)
    wa_y, wa_c = swap(own, t_mask=2), swap(own, t_mask=1)
    (n1,) = call(prep_kernel, "prep", [wide], [x, vecs])
    wu_y = swap(after(w_up, n1), t_mask=2)
    wd_y = swap(after(w_down, n1), t_mask=2)

    def attn_fwd(name, weights, hid, first=False, last=False):
        n = 128 * len(weights)
        shapes = [sds((rows, n))] * 4 + [sds((rows, 2 * n)), acc] + [wide] * last
        args = [scal, lengths, n1, hid, *weights, vecs]
        if first:
            shapes += [sds((D + BIAS, D)), sds((D, D)), sds((D, D)), sds((8, D), F32)]
            args += [w_up, w_down, cot]
        return call(
            functools.partial(attn_fwd_kernel, len(weights), first, last), name, shapes, args,
            [pltpu.SemaphoreType.DMA((5,))] if first else [], anywhere=(5, 7, 8) if first else (),
        )

    *saved_0, att0, pt0, hid, wa_c, u_own, d_own, csum = attn_fwd("attn_fwd_own", [own, wa_c], x, first=True)
    wa_y = after(wa_y, hid)
    wa_yc = swap(wa_y, t_mask=1)
    *saved_2, att2, pt2, hid = attn_fwd("attn_fwd_y", [wa_y], hid)
    wu_c, wd_c = swap(after(w_up, hid), t_mask=1), swap(after(w_down, hid), t_mask=1)
    *saved_3, att3, pt3, hid, n2 = attn_fwd("attn_fwd_yc", [wa_yc], hid, last=True)
    wa = [own, wa_c, wa_y, wa_yc]

    def part(n, *arrays, first=0, sums=True):
        return Part(n, [(v, first) for v in arrays], [(v, v.shape[0] - BIAS) for v in arrays] if sums else ())

    h, q = D // 2, D // 4
    bits = [1 << b for b in range(2, n_dp.bit_length() - 1)]

    def share(name, *args):
        first = len(args) == 3
        return call(
            functools.partial(share_kernel, first), name,
            [sds((D, D))] * 2 + [acc] * 2 + [sds((8, D), F32)] + ([] if first else [sds((D, D))]), [n2, cot, *args],
            [pltpu.VMEM((rows, D), BF)] * 2 + ([] if first else [pltpu.SemaphoreType.DMA((1,))]),
            anywhere=() if first else (7,),
        )

    def up(name, bias, u):
        return call(act_kernel, name, [wide, acc, sds((D, D))], [n2, cot, bias, u])

    def down(name, act, slope, u, d, *sums):
        return call(
            down_kernel, name, [sds((D, D))] + [acc] * 2 + [sds((8, D), F32)], [n2, cot, act, slope, u, d, *sums],
            [pltpu.VMEM((rows, D), BF)],
        )

    gu0, gd0, out_sum, dn2, bu0 = share("mlp_own", own, u_own, d_own)
    wu_y = after(wu_y, out_sum)
    wu_yc = swap(wu_y, t_mask=1)
    gu1, gd1, out_sum, dn2, bu1, wu_y = share("mlp_c", wa_c, wu_c, wd_c, out_sum, dn2, wu_y)
    gd1, gu1 = swap(gd1, t_mask=1), swap(gu1, t_mask=1)
    act3, slope3, gd3 = up("mlp_up_yc", wa_yc, wu_yc)
    gd3 = swap(gd3, t_mask=1)
    act2, slope2, gd2 = up("mlp_up_y", wa_y, wu_y)
    send, keep_d = combine("y", part(D, gd0, gd1, sums=False), part(D, gd2, gd3, sums=False), tag="d_y")
    got_d = swap(send, t_mask=2)
    wd_y = after(wd_y, send)
    wd_yc = swap(wd_y, t_mask=1)
    gu2, out_sum, dn2, bu2 = down("mlp_down_y", act2, slope2, wu_y, wd_y, out_sum, dn2)
    gu3, out_sum, dn2, bu3 = down("mlp_down_yc", act3, slope3, wu_yc, wd_yc, out_sum, dn2)
    gu3 = swap(gu3, t_mask=1)
    dh, gat, datt, sums2 = call(
        ln2_bwd_kernel, "ln2_bwd", [acc, wide, wide, sds((8, D), F32)], [hid, dn2, cot, vecs, *wa]
    )
    send, keep_u = combine("y", part(D, gu0, gu1, sums=False), part(D, gu2, gu3, sums=False), tag="u_y")
    got_u = swap(send, t_mask=2)
    send, keep_d = combine(0, part(D, keep_d, got_d, sums=False), tag="d_x")
    got_d = swap(send, dp_mask=1)
    dq, dk, dv = call(
        attn_core_bwd_kernel, "attn_core_bwd", [wide] * 3, [*saved_0, pt0, *saved_2, pt2, *saved_3, pt3, datt]
    )
    dn1, shared = call(
        attn_dx_kernel, "attn_dx", [acc, sds((8, D), F32)], [x, dq, dk, dv, sums2, csum, *wa]
    )

    def attn_dw(name, shapes, one, two, *atts):
        return call(functools.partial(attn_dw_kernel, one, two), name, shapes, [dq, dk, dv, n1, gat, shared, *atts])

    (got_a,) = attn_dw("attn_dw_sent", [sds((2 * (D + BIAS), D))], 1, 3, bu1, bu3, att0, att3)
    got_a = swap(got_a, t_mask=1)
    send, keep_u = combine(0, part(D, keep_u, got_u, sums=False), tag="u_x")
    got_u = swap(send, dp_mask=1)
    ga = attn_dw("attn_dw_kept", [sds((D + BIAS, D))] * 2, 0, 2, bu0, bu2, att0, att2)
    ab = lambda first, sums: [
        Part(h, [(ga[i], first), (got_a, i * (D + BIAS) + first)], [(ga[i], D), (got_a, i * (D + BIAS) + D)] if sums else ())
        for i in range(2)
    ]
    send, keep_d = combine(1, part(h, keep_d, got_d, sums=False), tag="d_z")
    got_d = swap(send, dp_mask=2)
    send, keep_l = combine("y", *ab(0, True), tag="l_y")
    got_l = swap(send, t_mask=2)
    send, keep_h = combine(0, *ab(h, False), tag="h_x")
    got_h = swap(send, dp_mask=1)
    def over_z(kind, *parts):
        parts = list(parts)
        for bit in bits:
            (one,) = combine("all", *parts, tag="all_" + kind)
            two = swap(one, dp_mask=bit)
            at, new = 0, []
            for p in parts:
                new.append(Part(p.n, [(v, at) for v in (one, two)], [(v, at + p.n) for v in (one, two)] if p.sums else ()))
                at += p.n + p.extra
            parts = new
            yield None
        yield combine("last", *parts, tag="last_" + kind)

    def gather(mine):
        return [mine] + [swap(mine, dp_mask=m) for m in (2, 1, 3)]

    def finish(kind, shapes, quarters):
        return call(
            functools.partial(final_kernel, kind), "final_" + kind, shapes, [scal, *quarters],
            [pltpu.VMEM((D, 128), F32)] if kind == "attn" else [],
        )

    def joined(mine, other, name):
        (half,) = call(join_kernel, name, [sds((2 * mine.shape[0], D))], [scal, mine, other], mib=8)
        return [half, swap(half, dp_mask=1)]

    def turn(z):
        for _ in bits:
            next(z)

    send, keep_u = combine(1, part(h, keep_u, got_u, sums=False), tag="u_z")
    got_u = swap(send, dp_mask=2)
    z_d = over_z("d", part(q, keep_d, got_d, sums=False))
    turn(z_d)
    (send_l, keep_l), (send_h, keep_h) = combine_all(
        (0, [part(h, keep_l, got_l)]), ("y", [Part(q, [(keep_h, i * q), (got_h, i * q)]) for i in range(2)]), tag="lxhy"
    )
    got_l, got_h = swap(send_l, dp_mask=1), swap(send_h, t_mask=2)
    z_u = over_z("u", part(q, keep_u, got_u, sums=False))
    turn(z_u)
    (mine_d,) = next(z_d)
    d_other = swap(mine_d, dp_mask=2)
    send, keep_a = combine(1, part(q, keep_l, got_l), part(q, keep_h, got_h, sums=False), tag="a_z")
    got_a = swap(send, dp_mask=2)
    all_d = joined(mine_d, d_other, "join_d")
    (mine_u,) = next(z_u)
    u_other = swap(mine_u, dp_mask=2)
    e = q // 2
    z_a = over_z(
        "a", Part(e, [(v, 0) for v in (keep_a, got_a)], [(v, e) for v in (keep_a, got_a)]),
        Part(e, [(v, e + BIAS) for v in (keep_a, got_a)]),
    )
    turn(z_a)
    grad_in, block_out = call(rows_kernel, "rows_out", [wide] * 2, [x, dh, dn1, hid, out_sum, vecs])
    all_u = joined(mine_u, u_other, "join_u")
    (grad_w_down,) = finish("down", [sds((D, D), F32)], all_d)
    mine_a, sums = next(z_a)
    all_a = gather(mine_a)
    (grad_w_up,) = finish("up", [sds((D, D), F32)], all_u)
    gwq, gwk, gwv, gwo = finish("attn", [sds((D, 128), F32)] * 3 + [sds((128, D), F32)], all_a)
    return (
        block_out, grad_in, sums[1], sums[2], gwq, sums[0, 0:128], gwk, gwv, sums[0, 256:384], gwo, sums[3],
        sums[4], sums[5], grad_w_up, sums[7], grad_w_down, sums[6],
    )


def solution(mesh):
    n_dp, n_t = mesh.shape["dp"], mesh.shape["tensor"]
    rows, cols, split, copied = P(("dp", "tensor"), None), P(None, "tensor"), P("tensor"), P()
    down = P("tensor", None)
    return jax.shard_map(
        functools.partial(layer, n_dp, n_t),
        mesh=mesh,
        in_specs=(
            rows, P("dp", None, None), copied, copied, cols, split, cols, cols, split, down, copied, copied, copied,
            cols, split, down, copied, rows,
        ),
        out_specs=(
            rows, rows, copied, copied, cols, split, cols, cols, split, down, copied, copied, copied, cols, split, down,
            copied,
        ),
        check_vma=False,
    )
```

```python
import functools

import jax
import jax.numpy as jnp
from jax import lax
from jax.experimental import pallas as pl
from jax.experimental.pallas import tpu as pltpu
from jax.sharding import PartitionSpec as P

BF, F32 = jnp.bfloat16, jnp.float32
D = 512
HD = 64
SLOT = 128
BR = 256
BIAS = 16
EPS = 1e-5
WEIGHTS = {"attn_dw_sent": 1, "attn_core_bwd": 1, "attn_dx": 1, "add_d_x": 0, "add_ud_x": 0, "add_l_y": 0, "add_h_x": 0, "add_lyhx": 0, "add_u_y": 0, "add_last_d": 0, "rows_out": 1}
LN1_G, LN1_B, B_OUT, LN2_G, LN2_B, B_DOWN, B_UP, B_QV = range(8)
SMEM = functools.partial(pl.BlockSpec, memory_space=pltpu.SMEM)
VMEM = functools.partial(pl.BlockSpec, memory_space=pltpu.VMEM)


def dot(a, b):
    return lax.dot_general(a, b, (((1,), (0,)), ((), ())), preferred_element_type=F32)


def dot_nt(a, b):
    return lax.dot_general(a, b, (((1,), (1,)), ((), ())), preferred_element_type=F32)


def dot_tn(a, b):
    return lax.dot_general(a, b, (((0,), (0,)), ((), ())), preferred_element_type=F32)


def params(mib, **kw):
    return pltpu.CompilerParams(vmem_limit_bytes=mib << 20, **kw)


def cost(flops, nbytes, trans=0):
    return pl.CostEstimate(flops=int(flops), bytes_accessed=int(nbytes), transcendentals=int(trans))


def sds(shape, dtype=BF):
    return jax.ShapeDtypeStruct(shape, dtype)


def fetch(src, dst, sems, at=0, pieces=4):
    n = dst.shape[0] // pieces
    copies = [
        pltpu.make_async_copy(src.at[i * n : (i + 1) * n, :], dst.at[i * n : (i + 1) * n, :], sems.at[at + i])
        for i in range(pieces)
    ]
    for c in copies:
        c.start()
    return copies


def await_all(*groups):
    for group in groups:
        for c in group:
            c.wait()


def normalise(v):
    mean = jnp.mean(v, -1, keepdims=True)
    centred = v - mean
    rstd = lax.rsqrt(jnp.mean(centred * centred, -1, keepdims=True) + EPS)
    return centred * rstd, rstd


def head_stack(v):
    first = lax.broadcasted_iota(jnp.int32, v.shape, 1) < HD
    zero = jnp.zeros_like(v)
    return jnp.concatenate([jnp.where(first, v, zero), jnp.where(first, zero, v)], 0)


def untranspose(v):
    return jnp.concatenate([v[:, :SLOT].T, v[:, SLOT:].T], 1)


def slot_bias(len1, len2):
    def places(shape, dim):
        p = lax.broadcasted_iota(jnp.int32, shape, dim) & (SLOT - 1)
        second = (p >= SLOT // 2) & (len2 > 0)
        local = jnp.where(second, p - SLOT // 2, p)
        valid = local < jnp.where(second, len2, len1)
        base = jnp.where(second, 1000, 0)
        return valid, base, base + ((local * 43) >> 8)

    valid_k, _, frame_k = places((SLOT, 1), 0)
    valid_q, base_q, frame_q = places((1, 2 * SLOT), 1)
    frame_k = jnp.where(valid_k, frame_k, 1 << 20)
    frame_q = jnp.where(valid_q, frame_q, -1)
    allowed = (frame_k <= frame_q) & (frame_k >= base_q)
    return jnp.where(allowed, 0.0, -1e30).astype(F32)


def pack_kernel(*refs):
    wq, wk, wv, wo = refs[:4]
    small, (out, vecs), held, sems = refs[4:13], refs[13:15], refs[15:24], refs[24]
    copies = [pltpu.make_async_copy(v, h, sems.at[7 + i]) for i, (v, h) in enumerate(zip(small, held))]
    for i, ref in enumerate((wq, wk, wv)):
        copies.append(pltpu.make_async_copy(ref, out.at[0:D, i * 128 : (i + 1) * 128], sems.at[i]))
    for b in range(4):
        blk = slice(b * 128, (b + 1) * 128)
        copies.append(pltpu.make_async_copy(wo.at[:, blk], out.at[blk, 384:512], sems.at[3 + b]))
    for c in copies:
        c.start()
    for c in copies[: len(small)]:
        c.wait()
    rows = [h[...].astype(F32).reshape(1, h.shape[0]) for h in held]
    gap = jnp.zeros((1, 128), F32)
    rows[7:] = [jnp.concatenate([rows[7], gap, rows[8], gap], 1)]
    table = jnp.concatenate(rows, 0)
    vecs[...] = table
    row = lax.broadcasted_iota(jnp.int32, (BIAS, D), 0)
    block = jnp.where(row == 0, table[B_QV : B_QV + 1], jnp.where(row == 1, table[B_UP : B_UP + 1], 0.0))
    out[D : D + BIAS, :] = block.astype(BF)
    for c in copies[len(small) :]:
        c.wait()


def prep_kernel(x, vecs, n1_o):
    def tile(m, _):
        here = pl.ds(pl.multiple_of(m * BR, BR), BR)
        xhat, _ = normalise(x[here, :].astype(F32))
        n1_o[here, :] = (xhat * vecs[LN1_G : LN1_G + 1, :] + vecs[LN1_B : LN1_B + 1, :]).astype(BF)
        return 0

    lax.fori_loop(0, x.shape[0] // BR, tile, 0, unroll=2)


def attn_fwd_kernel(shares, first, last, *refs):
    (scal, lens, n1, base), w = refs[:4], list(refs[4 : 4 + shares])
    vecs, (q_o, k_o, v_o, att_o, pt_o, hid_o), n2_o = refs[4 + shares], refs[5 + shares + 3 * first : 11 + shares + 3 * first], refs[-1]
    if first:
        up_in, down_in, cot, wa_o, up_o, down_o, csum_o, sems = *refs[7:10], *refs[-5:]
        fetched = fetch(w[1], wa_o, sems, pieces=3)
        brought = [pltpu.make_async_copy(up_in, up_o, sems.at[3]), pltpu.make_async_copy(down_in, down_o, sems.at[4])]
        for c in brought:
            c.start()
        await_all(fetched)
        w[1] = wa_o
    slots = n1.shape[0] // SLOT

    for c in range(shares):
        brow = w[c][D : D + BIAS, :].astype(F32)[0:1]
        cols = slice(c * 128, (c + 1) * 128)
        qkv = dot(n1[...], w[c][0:D, 0:384])
        q_o[:, cols] = (qkv[:, 0:128] + brow[:, 0:128]).astype(BF) * jnp.asarray(0.125, BF)
        k_o[:, cols] = qkv[:, 128:256].astype(BF)
        v_o[:, cols] = (qkv[:, 256:384] + brow[:, 256:384]).astype(BF)

    def slot(s, _):
        rows = pl.ds(pl.multiple_of(s * SLOT, SLOT), SLOT)
        place = scal[3] + s
        mask = slot_bias(lens[0, place, 0], lens[0, place, 1])
        for c in range(shares):
            cols = slice(c * 128, (c + 1) * 128)
            st = dot_nt(k_o[rows, cols], head_stack(q_o[rows, cols])) + mask
            top = jnp.maximum(jnp.max(st, 0, keepdims=True), -1e29)
            e = jnp.exp(st - top)
            den = jnp.sum(e, 0, keepdims=True)
            pt = (e * (1.0 / jnp.where(den == 0.0, 1.0, den))).astype(BF)
            pt_o[rows, c * 256 : (c + 1) * 256] = pt
            att_o[rows, cols] = dot(untranspose(pt), head_stack(v_o[rows, cols])).astype(BF)
        return 0

    lax.fori_loop(0, slots, slot, 0, unroll=True)
    hid = base[...].astype(F32)
    if first:
        hid += vecs[B_OUT : B_OUT + 1, :]
    for c in range(shares):
        wo = jnp.concatenate([w[c][b * 128 : (b + 1) * 128, 384:512] for b in range(4)], 1)
        hid += dot(att_o[:, c * 128 : (c + 1) * 128], wo)
    hid_o[...] = hid
    if first:
        csum_o[...] = jnp.broadcast_to(jnp.sum(cot[...].astype(F32), 0, keepdims=True), (8, D))
        await_all(brought)
    if last:

        def tile(m, _):
            here = pl.ds(pl.multiple_of(m * BR, BR), BR)
            xhat, _ = normalise(hid_o[here, :])
            n2_o[here, :] = (xhat * vecs[LN2_G : LN2_G + 1, :] + vecs[LN2_B : LN2_B + 1, :]).astype(BF)
            return 0

        lax.fori_loop(0, n1.shape[0] // BR, tile, 0, unroll=2)


def gelu_pair(u):
    phi = 0.5 + 0.5 * lax.erf(u * 0.7071067811865476)
    return u * phi, phi + u * (jnp.exp(-0.5 * (u * u)) * 0.3989422804014327)


def share_kernel(first, n2, cot, wa, u, d, *refs):
    if not first:
        out_i, dn2_i, up_in, refs, (up_o, act_s, gup_s, sem) = *refs[:3], refs[3:8], refs[8:]
        brought = pltpu.make_async_copy(up_in, up_o, sem.at[0])
        brought.start()
    else:
        act_s, gup_s = refs[5:]
    gu_o, gd_o, out, dn2, bu_o = refs[:5]
    bias = wa[D : D + BIAS, :].astype(F32)[1:2]

    def tile(m, sums):
        here = pl.ds(pl.multiple_of(m * BR, BR), BR)
        n, c = n2[here, :], cot[here, :]
        up = dot(n, u[...]) + bias
        dact = dot_nt(c, d[...])
        act, slope = gelu_pair(up)
        gup = (slope * dact).astype(BF)
        act = act.astype(BF)
        act_s[here, :] = act
        gup_s[here, :] = gup
        o, e = dot(act, d[...]), dot_nt(gup, u[...])
        out[here, :] = o if first else out_i[here, :] + o
        dn2[here, :] = e if first else dn2_i[here, :] + e
        return sums + jnp.sum(gup.astype(F32), 0, keepdims=True)

    sums = lax.fori_loop(0, n2.shape[0] // BR, tile, jnp.zeros((1, D), F32), unroll=True)
    gu_o[...] = dot_tn(n2[...], gup_s[...]).astype(BF)
    gd_o[...] = dot_tn(cot[...], act_s[...]).astype(BF)
    bu_o[...] = jnp.broadcast_to(sums, (8, D))
    if not first:
        brought.wait()


def act_kernel(n2, cot, bias, u, act_o, slope_o, gd_o):
    add = bias[D : D + BIAS, :].astype(F32)[1:2]

    def tile(m, _):
        here = pl.ds(pl.multiple_of(m * BR, BR), BR)
        act, slope = gelu_pair(dot(n2[here, :], u[...]) + add)
        act_o[here, :] = act.astype(BF)
        slope_o[here, :] = slope
        return 0

    lax.fori_loop(0, n2.shape[0] // BR, tile, 0, unroll=True)
    gd_o[...] = dot_tn(cot[...], act_o[...]).astype(BF)


def down_kernel(n2, cot, act, slope, u, d, out_i, dn2_i, gu_o, out, dn2, bu_o, gup_s):
    def tile(m, sums):
        here = pl.ds(pl.multiple_of(m * BR, BR), BR)
        gup = (slope[here, :] * dot_nt(cot[here, :], d[...])).astype(BF)
        gup_s[here, :] = gup
        out[here, :] = out_i[here, :] + dot(act[here, :], d[...])
        dn2[here, :] = dn2_i[here, :] + dot_nt(gup, u[...])
        return sums + jnp.sum(gup.astype(F32), 0, keepdims=True)

    sums = lax.fori_loop(0, n2.shape[0] // BR, tile, jnp.zeros((1, D), F32), unroll=True)
    gu_o[...] = dot_tn(n2[...], gup_s[...]).astype(BF)
    bu_o[...] = jnp.broadcast_to(sums, (8, D))


def total(sums, *adds):
    return sums + jnp.concatenate([jnp.sum(a, 0, keepdims=True) for a in adds], 0)


def ln2_bwd_kernel(hid, dn2, cot, vecs, *refs):
    w, (dh_o, gat_s, datt_o, sums_o) = refs[:4], refs[4:]
    rows = hid.shape[0]

    def tile(m, sums):
        here = pl.ds(pl.multiple_of(m * BR, BR), BR)
        xhat, rstd = normalise(hid[here, :])
        dn = dn2[here, :]
        e = dn * vecs[LN2_G : LN2_G + 1, :]
        cotf = cot[here, :].astype(F32)
        dh = cotf + rstd * (e - jnp.mean(e, -1, keepdims=True) - xhat * jnp.mean(e * xhat, -1, keepdims=True))
        dh_o[here, :] = dh
        gat = dh.astype(BF)
        gat_s[here, :] = gat
        return total(sums, gat.astype(F32), dn * xhat, dn)

    sums_o[0:3, :] = lax.fori_loop(0, rows // BR, tile, jnp.zeros((3, D), F32), unroll=2)
    sums_o[3:8, :] = jnp.zeros((5, D), F32)
    for c in range(4):
        wo = jnp.concatenate([w[c][b * 128 : (b + 1) * 128, 384:512] for b in range(4)], 1)
        datt_o[:, c * 128 : (c + 1) * 128] = dot_nt(gat_s[...], wo).astype(BF)


def attn_core_bwd_kernel(*refs):
    saved, (datt, dq_o, dk_o, dv_o) = refs[:12], refs[12:]
    where = ((0, 0), (0, 1), (1, 0), (2, 0))

    def slot(s, _):
        rows = pl.ds(pl.multiple_of(s * SLOT, SLOT), SLOT)
        held = []
        for c, (group, at) in enumerate(where):
            q, k, v, pt_r = saved[4 * group : 4 * group + 4]
            cols = slice(at * 128, (at + 1) * 128)
            out = slice(c * 128, (c + 1) * 128)
            das = head_stack(datt[rows, out])
            pt = pt_r[rows, at * 256 : (at + 1) * 256]
            dpt = dot_nt(v[rows, cols], das)
            dv_o[rows, out] = dot(pt, das).astype(BF)
            held.append((q, k, cols, out, pt, dpt))
        ready = []
        for q, k, cols, out, pt, dpt in held:
            ptf = pt.astype(F32)
            delta = jnp.sum(ptf * dpt, 0, keepdims=True)
            ds = (ptf * (dpt - delta)).astype(BF)
            ready.append((q, k, cols, out, ds, untranspose(ds)))
        for q, k, cols, out, ds, dst in ready:
            dq_o[rows, out] = (dot(dst, head_stack(k[rows, cols])) * 0.125).astype(BF)
            dk_o[rows, out] = dot(ds, head_stack(q[rows, cols])).astype(BF)
        return 0

    lax.fori_loop(0, datt.shape[0] // SLOT, slot, 0, unroll=True)


def attn_dw_kernel(one, two, dq, dk, dv, n1, gat, shared, bu_one, bu_two, att_one, att_two, *ga):
    gap = jnp.zeros((1, 128), F32)
    grads = [[s[:, c * 128 : (c + 1) * 128] for s in (dq, dk, dv)] for c in (one, two)]
    sums = [[jnp.sum(g[j].astype(F32), 0, keepdims=True) for j in (0, 2)] for g in grads]
    g = dot_tn(n1[...], jnp.concatenate(grads[0] + grads[1], 1)).astype(BF)
    att = [a[...] if a.shape[1] == 128 else a[:, (c % 2) * 128 : (c % 2 + 1) * 128] for a, c in zip((att_one, att_two), (one, two))]
    go = dot_tn(gat[...], jnp.concatenate(att, 1)).astype(BF)
    for i in range(2):
        o, at = ga[i % len(ga)], 0 if len(ga) == 2 else i * (D + BIAS)
        o[at : at + D, 0:384] = g[:, i * 384 : (i + 1) * 384]
        o[at : at + D, 384:512] = go[:, i * 128 : (i + 1) * 128]
        own = jnp.concatenate([sums[i][0], gap, sums[i][1], gap], 1)
        o[at + D : at + D + BIAS, :] = bias_block(jnp.concatenate([own, shared[0:6, :], (bu_one, bu_two)[i][0:1, :]], 0))


def attn_dx_kernel(x, dq, dk, dv, sums2, csum, *refs):
    w, (dn1_o, shared_o) = refs[:4], refs[4:]

    def tile(m, sums):
        here = pl.ds(pl.multiple_of(m * BR, BR), BR)
        dn1 = None
        for c in range(4):
            cols = slice(c * 128, (c + 1) * 128)
            grads = jnp.concatenate([dq[here, cols], dk[here, cols], dv[here, cols]], 1)
            part = dot_nt(grads, w[c][0:D, 0:384])
            dn1 = part if dn1 is None else dn1 + part
        dn1_o[here, :] = dn1
        xhat, _ = normalise(x[here, :].astype(F32))
        return total(sums, dn1 * xhat, dn1)

    sums1 = lax.fori_loop(0, x.shape[0] // BR, tile, jnp.zeros((2, D), F32), unroll=True)
    shared_o[...] = jnp.concatenate([sums1, sums2[0:3, :], csum[0:1, :], jnp.zeros((2, D), F32)], 0)


def rows_kernel(x, dh, dn1, hid, mlp, vecs, gin_o, block_o):
    def tile(m, _):
        here = pl.ds(pl.multiple_of(m * BR, BR), BR)
        xhat, rstd = normalise(x[here, :].astype(F32))
        e = dn1[here, :] * vecs[LN1_G : LN1_G + 1, :]
        back = rstd * (e - jnp.mean(e, -1, keepdims=True) - xhat * jnp.mean(e * xhat, -1, keepdims=True))
        gin_o[here, :] = (dh[here, :] + back).astype(BF)
        block_o[here, :] = (hid[here, :] + mlp[here, :] + vecs[B_DOWN : B_DOWN + 1, :]).astype(BF)
        return 0

    lax.fori_loop(0, x.shape[0] // BR, tile, 0, unroll=2)


def bias_block(total):
    high = total.astype(BF)
    return jnp.concatenate([high, (total - high.astype(F32)).astype(BF)], 0)


class Part:
    def __init__(self, n, sources, sums=()):
        self.n, self.sources, self.sums = n, sources, sums
        self.extra = BIAS if sums else 0


def combine_kernel(groups, *refs):
    scal, ins = refs[0], refs[1:]
    n_in = 1 + max(i for _, parts in groups for part in parts for i, _ in part[1] + part[2])
    ins, rest = ins[:n_in], list(ins[n_in:])

    def summed(part, start, size):
        acc = None
        for i, first in part[1]:
            v = ins[i][pl.ds(first + start, size), :].astype(F32)
            acc = v if acc is None else acc + v
        return acc.astype(BF)

    def sums(part):
        rows = [ins[i][first : first + BIAS, :].astype(F32) for i, first in part[2]]
        terms = [v[0:8] + v[8:16] for v in rows]
        while len(terms) > 1:
            terms = [sum(terms[i + 1 : i + 2], terms[i]) for i in range(0, len(terms), 2)]
        return terms[0]

    for op, parts in groups:
        if op == "y":
            for part in (parts[1], parts[0]):
                o, n = rest.pop(0), part[0]
                o[0:n, :] = summed(part, 0, n)
                if part[2]:
                    o[n : n + BIAS, :] = bias_block(sums(part))
            continue
        outs = [rest.pop(0) for _ in range(1 if op in ("all", "last") else 2)]
        at = 0
        for part in parts:
            n, biased = part[0], bool(part[2])
            if op in ("all", "last"):
                outs[0][at : at + n, :] = summed(part, 0, n)
                at += n
                if biased and op == "last":
                    rest.pop(0)[...] = sums(part)
                elif biased:
                    outs[0][at : at + BIAS, :] = bias_block(sums(part))
                    at += BIAS
            else:
                bit, h = scal[op], n // 2
                outs[0][at : at + h, :] = summed(part, pl.multiple_of((1 - bit) * h, h), h)
                outs[1][at : at + h, :] = summed(part, pl.multiple_of(bit * h, h), h)
                at += h
                if biased:
                    block = bias_block(sums(part))
                    for o in outs:
                        o[at : at + BIAS, :] = block
                    at += BIAS


def join_kernel(scal, mine, other, out):
    bit, n = scal[1], mine.shape[0]
    out[pl.ds(pl.multiple_of(bit * n, n), n), :] = mine[...]
    out[pl.ds(pl.multiple_of((1 - bit) * n, n), n), :] = other[...]


def final_kernel(kind, *refs):
    scal, outs = refs[0], refs[-1:] if kind != "attn" else refs[-5:]
    got = refs[1 : len(refs) - len(outs)]
    x, z = scal[0], scal[1]
    if len(got) == 2:
        places = (x, 1 - x)
    else:
        places = (x * 2 + z, x * 2 + 1 - z, (1 - x) * 2 + z, (1 - x) * 2 + 1 - z)
    halves = 2 if kind == "attn" else 1
    n = got[0].shape[0] // halves
    for half in range(halves):
        for place, ref in zip(places, got):
            at = pl.ds(pl.multiple_of(half * 4 * n + place * n, n), n)
            v = ref[half * n : (half + 1) * n, :].astype(F32)
            if kind == "up":
                outs[0][at, :] = v
            elif kind == "down":
                outs[0][:, at] = v.T
            else:
                for j in range(3):
                    outs[j][at, :] = v[:, j * 128 : (j + 1) * 128]
                outs[4][at, :] = v[:, 384:512]
    if kind == "attn":
        outs[3][...] = outs[4][...].T


def attn_final_kernel(scal, *refs):
    sums, outs = refs[4], refs[5:]
    final_kernel("attn", scal, *refs[0:4], *outs[0:4], outs[-1])
    outs[4][...] = sums[0:1, 0:128].reshape(128)
    outs[5][...] = sums[0:1, 256:384].reshape(128)
    for i in range(7):
        outs[6 + i][...] = sums[i + 1 : i + 2, :].reshape(D)


def layer(
    n_dp, n_t, x, lengths, ln1_gain, ln1_bias, w_query, b_query, w_key, w_value, b_value, w_out, b_out,
    ln2_gain, ln2_bias, w_up, b_up, w_down, b_down, cot,
):
    rows = x.shape[0]
    dp_at, t_at = lax.axis_index("dp"), lax.axis_index("tensor")
    scal = jnp.stack([dp_at & 1, (dp_at >> 1) & 1, t_at, t_at * (rows // SLOT)]).astype(jnp.int32)
    last = [scal]

    class Swap:
        def __init__(self, v, dp_mask=0, t_mask=0):
            self.v, self.masks, self.shape, self.made = v, (dp_mask, t_mask), v.shape, None

        def get(self):
            if self.made is None:
                self.made = swap_now(self.v, *self.masks)
            return self.made

    def real(v):
        return v.get() if isinstance(v, Swap) else v

    def swap(v, dp_mask=0, t_mask=0):
        return Swap(real(v), dp_mask, t_mask)

    def swap_now(v, dp_mask=0, t_mask=0):
        pairs = [(d * n_t + t, (d ^ dp_mask) * n_t + (t ^ t_mask)) for d in range(n_dp) for t in range(n_t)]
        return lax.ppermute(v, ("dp", "tensor"), pairs)

    def after(v, *tokens):
        return lax.optimization_barrier((real(v), *tokens))[0]

    def hbm(v):
        return pltpu.with_memory_space_constraint(v, pltpu.HBM)

    def call(kernel, name, out_shape, args, scratch=(), mib=16, in_hbm=False, weight=10, anywhere=()):
        args = [real(a) for a in args]
        if last[0] is not scal:
            i = max((j for j in range(len(args)) if j not in anywhere), key=lambda j: args[j].size)
            args[i] = after(args[i], last[0])
        specs = [SMEM() if a.dtype == jnp.int32 else VMEM() for a in args]
        for j in anywhere:
            specs[j] = pl.BlockSpec(memory_space=pl.ANY)
        if in_hbm:
            args = [hbm(a) for a in args]
            specs = [pl.BlockSpec(memory_space=pltpu.HBM)] * len(args)
        out = pl.pallas_call(
            kernel,
            out_shape=out_shape,
            in_specs=specs,
            out_specs=[VMEM()] * len(out_shape),
            scratch_shapes=list(scratch),
            compiler_params=params(mib),
            cost_estimate=cost(WEIGHTS.get(name, weight) * 10**9, 10**8),
            name=name,
        )(*args)
        last[0] = min(out, key=lambda o: o.size)
        return out

    def combine_all(*groups, tag):
        arrays, spec, shapes, counts = [], [], [], []
        for op, parts in groups:
            for p in parts:
                for array, _ in (*p.sources, *p.sums):
                    if not any(real(array) is known for known in arrays):
                        arrays.append(real(array))
        place = lambda array: next(i for i, known in enumerate(arrays) if known is real(array))
        for op, parts in groups:
            spec.append((op, tuple((p.n, *(tuple((place(v), at) for v, at in w) for w in (p.sources, p.sums))) for p in parts)))
            if op == "y":
                new = [sds((p.n + p.extra, D)) for p in (parts[1], parts[0])]
            elif op == "all":
                new = [sds((sum(p.n + p.extra for p in parts), D))]
            elif op == "last":
                new = [sds((sum(p.n for p in parts), D))] + [sds((8, D), F32) for p in parts if p.sums]
            else:
                new = [sds((sum(p.n // 2 + p.extra for p in parts), D))] * 2
            shapes += new
            counts.append(len(new))
        out = list(call(functools.partial(combine_kernel, tuple(spec)), "add_" + tag, shapes, [scal, *arrays], mib=8))
        return [[out.pop(0) for _ in range(n)] for n in counts]

    def combine(op, *parts, tag):
        return combine_all((op, parts), tag=tag)[0]

    own, vecs = call(
        pack_kernel, "pack", [sds((D + BIAS, D)), sds((8, D), F32)],
        [w_query, w_key, w_value, w_out, ln1_gain, ln1_bias, b_out, ln2_gain, ln2_bias, b_down, b_up, b_query, b_value],
        [pltpu.VMEM((D,), F32)] * 2 + [pltpu.VMEM((D,), BF)] + [pltpu.VMEM((D,), F32)] * 2 + [pltpu.VMEM((D,), BF)] * 2
        + [pltpu.VMEM((128,), BF)] * 2 + [pltpu.SemaphoreType.DMA((16,))],
        in_hbm=True,
    )
    wide, acc = sds((rows, D)), sds((rows, D), F32)
    wa_y, wa_c = swap(own, t_mask=2), swap(own, t_mask=1)
    (n1,) = call(prep_kernel, "prep", [wide], [x, vecs])
    wu_y = swap(after(w_up, n1), t_mask=2)
    wd_y = swap(after(w_down, n1), t_mask=2)

    def attn_fwd(name, weights, hid, first=False, last=False):
        n = 128 * len(weights)
        shapes = [sds((rows, n))] * 4 + [sds((rows, 2 * n)), acc] + [wide] * last
        args = [scal, lengths, n1, hid, *weights, vecs]
        if first:
            shapes += [sds((D + BIAS, D)), sds((D, D)), sds((D, D)), sds((8, D), F32)]
            args += [w_up, w_down, cot]
        return call(
            functools.partial(attn_fwd_kernel, len(weights), first, last), name, shapes, args,
            [pltpu.SemaphoreType.DMA((5,))] if first else [], anywhere=(5, 7, 8) if first else (),
        )

    *saved_0, att0, pt0, hid, wa_c, u_own, d_own, csum = attn_fwd("attn_fwd_own", [own, wa_c], x, first=True)
    wa_y = after(wa_y, hid)
    wa_yc = swap(wa_y, t_mask=1)
    *saved_2, att2, pt2, hid = attn_fwd("attn_fwd_y", [wa_y], hid)
    wu_c, wd_c = swap(after(w_up, hid), t_mask=1), swap(after(w_down, hid), t_mask=1)
    *saved_3, att3, pt3, hid, n2 = attn_fwd("attn_fwd_yc", [wa_yc], hid, last=True)
    wa = [own, wa_c, wa_y, wa_yc]

    def part(n, *arrays, first=0, sums=True):
        return Part(n, [(v, first) for v in arrays], [(v, v.shape[0] - BIAS) for v in arrays] if sums else ())

    h, q = D // 2, D // 4
    bits = [1 << b for b in range(2, n_dp.bit_length() - 1)]

    def share(name, *args):
        first = len(args) == 3
        return call(
            functools.partial(share_kernel, first), name,
            [sds((D, D))] * 2 + [acc] * 2 + [sds((8, D), F32)] + ([] if first else [sds((D, D))]), [n2, cot, *args],
            [pltpu.VMEM((rows, D), BF)] * 2 + ([] if first else [pltpu.SemaphoreType.DMA((1,))]),
            anywhere=() if first else (7,),
        )

    def up(name, bias, u):
        return call(act_kernel, name, [wide, acc, sds((D, D))], [n2, cot, bias, u])

    def down(name, act, slope, u, d, *sums):
        return call(
            down_kernel, name, [sds((D, D))] + [acc] * 2 + [sds((8, D), F32)], [n2, cot, act, slope, u, d, *sums],
            [pltpu.VMEM((rows, D), BF)],
        )

    gu0, gd0, out_sum, dn2, bu0 = share("mlp_own", own, u_own, d_own)
    wu_y = after(wu_y, out_sum)
    wu_yc = swap(wu_y, t_mask=1)
    gu1, gd1, out_sum, dn2, bu1, wu_y = share("mlp_c", wa_c, wu_c, wd_c, out_sum, dn2, wu_y)
    gd1, gu1 = swap(gd1, t_mask=1), swap(gu1, t_mask=1)
    act3, slope3, gd3 = up("mlp_up_yc", wa_yc, wu_yc)
    gd3 = swap(gd3, t_mask=1)
    act2, slope2, gd2 = up("mlp_up_y", wa_y, wu_y)
    send, keep_d = combine("y", part(D, gd0, gd1, sums=False), part(D, gd2, gd3, sums=False), tag="d_y")
    got_d = swap(send, t_mask=2)
    wd_y = after(wd_y, send)
    wd_yc = swap(wd_y, t_mask=1)
    gu2, out_sum, dn2, bu2 = down("mlp_down_y", act2, slope2, wu_y, wd_y, out_sum, dn2)
    gu3, out_sum, dn2, bu3 = down("mlp_down_yc", act3, slope3, wu_yc, wd_yc, out_sum, dn2)
    gu3 = swap(gu3, t_mask=1)
    dh, gat, datt, sums2 = call(
        ln2_bwd_kernel, "ln2_bwd", [acc, wide, wide, sds((8, D), F32)], [hid, dn2, cot, vecs, *wa]
    )
    send, keep_u = combine("y", part(D, gu0, gu1, sums=False), part(D, gu2, gu3, sums=False), tag="u_y")
    got_u = swap(send, t_mask=2)
    send, keep_d = combine(0, part(D, keep_d, got_d, sums=False), tag="d_x")
    got_d = swap(send, dp_mask=1)
    dq, dk, dv = call(
        attn_core_bwd_kernel, "attn_core_bwd", [wide] * 3, [*saved_0, pt0, *saved_2, pt2, *saved_3, pt3, datt]
    )
    dn1, shared = call(
        attn_dx_kernel, "attn_dx", [acc, sds((8, D), F32)], [x, dq, dk, dv, sums2, csum, *wa]
    )

    def attn_dw(name, shapes, one, two, *atts):
        return call(functools.partial(attn_dw_kernel, one, two), name, shapes, [dq, dk, dv, n1, gat, shared, *atts])

    (got_a,) = attn_dw("attn_dw_sent", [sds((2 * (D + BIAS), D))], 1, 3, bu1, bu3, att0, att3)
    got_a = swap(got_a, t_mask=1)
    send, keep_u = combine(0, part(D, keep_u, got_u, sums=False), tag="u_x")
    got_u = swap(send, dp_mask=1)
    ga = attn_dw("attn_dw_kept", [sds((D + BIAS, D))] * 2, 0, 2, bu0, bu2, att0, att2)
    ab = lambda first, sums: [
        Part(h, [(ga[i], first), (got_a, i * (D + BIAS) + first)], [(ga[i], D), (got_a, i * (D + BIAS) + D)] if sums else ())
        for i in range(2)
    ]
    send, keep_d = combine(1, part(h, keep_d, got_d, sums=False), tag="d_z")
    got_d = swap(send, dp_mask=2)
    send, keep_l = combine("y", *ab(0, True), tag="l_y")
    got_l = swap(send, t_mask=2)
    send, keep_h = combine(0, *ab(h, False), tag="h_x")
    got_h = swap(send, dp_mask=1)
    def over_z(kind, *parts):
        parts = list(parts)
        for bit in bits:
            (one,) = combine("all", *parts, tag="all_" + kind)
            two = swap(one, dp_mask=bit)
            at, new = 0, []
            for p in parts:
                new.append(Part(p.n, [(v, at) for v in (one, two)], [(v, at + p.n) for v in (one, two)] if p.sums else ()))
                at += p.n + p.extra
            parts = new
            yield None
        yield combine("last", *parts, tag="last_" + kind)

    def gather(mine):
        return [mine] + [swap(mine, dp_mask=m) for m in (2, 1, 3)]

    def finish(kind, shapes, quarters):
        return call(
            functools.partial(final_kernel, kind), "final_" + kind, shapes, [scal, *quarters],
            [pltpu.VMEM((D, 128), F32)] if kind == "attn" else [],
        )

    def joined(mine, other, name):
        (half,) = call(join_kernel, name, [sds((2 * mine.shape[0], D))], [scal, mine, other], mib=8)
        return [half, swap(half, dp_mask=1)]

    def turn(z):
        for _ in bits:
            next(z)

    send, keep_u = combine(1, part(h, keep_u, got_u, sums=False), tag="u_z")
    got_u = swap(send, dp_mask=2)
    z_d = over_z("d", part(q, keep_d, got_d, sums=False))
    turn(z_d)
    (send_l, keep_l), (send_h, keep_h) = combine_all(
        (0, [part(h, keep_l, got_l)]), ("y", [Part(q, [(keep_h, i * q), (got_h, i * q)]) for i in range(2)]), tag="lxhy"
    )
    got_l, got_h = swap(send_l, dp_mask=1), swap(send_h, t_mask=2)
    z_u = over_z("u", part(q, keep_u, got_u, sums=False))
    turn(z_u)
    (mine_d,) = next(z_d)
    d_other = swap(mine_d, dp_mask=2)
    send, keep_a = combine(1, part(q, keep_l, got_l), part(q, keep_h, got_h, sums=False), tag="a_z")
    got_a = swap(send, dp_mask=2)
    all_d = joined(mine_d, d_other, "join_d")
    (mine_u,) = next(z_u)
    u_other = swap(mine_u, dp_mask=2)
    e = q // 2
    z_a = over_z(
        "a", Part(e, [(v, 0) for v in (keep_a, got_a)], [(v, e) for v in (keep_a, got_a)]),
        Part(e, [(v, e + BIAS) for v in (keep_a, got_a)]),
    )
    turn(z_a)
    grad_in, block_out = call(rows_kernel, "rows_out", [wide] * 2, [x, dh, dn1, hid, out_sum, vecs])
    all_u = joined(mine_u, u_other, "join_u")
    (grad_w_down,) = finish("down", [sds((D, D), F32)], all_d)
    mine_a, sums = next(z_a)
    all_a = gather(mine_a)
    (grad_w_up,) = finish("up", [sds((D, D), F32)], all_u)
    vec, short = sds((D,), F32), sds((128,), F32)
    gwq, gwk, gwv, gwo, gbq, gbv, *vectors = call(
        attn_final_kernel, "final_attn", [sds((D, 128), F32)] * 3 + [sds((128, D), F32)] + [short] * 2 + [vec] * 7,
        [scal, *all_a, sums], [pltpu.VMEM((D, 128), F32)],
    )
    ln1_g, ln1_b, b_o, ln2_g, ln2_b, b_d, b_u = vectors
    return (
        block_out, grad_in, ln1_g, ln1_b, gwq, gbq, gwk, gwv, gbv, gwo, b_o, ln2_g, ln2_b, grad_w_up, b_u, grad_w_down, b_d,
    )


def solution(mesh):
    n_dp, n_t = mesh.shape["dp"], mesh.shape["tensor"]
    rows, cols, split, copied = P(("dp", "tensor"), None), P(None, "tensor"), P("tensor"), P()
    down = P("tensor", None)
    return jax.shard_map(
        functools.partial(layer, n_dp, n_t),
        mesh=mesh,
        in_specs=(
            rows, P("dp", None, None), copied, copied, cols, split, cols, cols, split, down, copied, copied, copied,
            cols, split, down, copied, rows,
        ),
        out_specs=(
            rows, rows, copied, copied, cols, split, cols, cols, split, down, copied, copied, copied, cols, split, down,
            copied,
        ),
        check_vma=False,
    )
```
